256 devices in a mesh: qrow: 16 (over z, x_hi), kcol: 16 (over y, x_lo, core).
Axes of the slice: x: 4 (x_hi: 2, x_lo: 2; x = x_hi * 2 + x_lo), y: 4, z: 8, core: 2. Of those that a mesh axis runs over, the one named last changes fastest.
Arguments:
- query_latent: bfloat16 [1024, 65536], P('qrow', 'kcol'), may hold values from -40 to 40
- query_rope: bfloat16 [1024, 8192], P('qrow', 'kcol'), may hold values from -6 to 6
- code_latent: bfloat16 [16384, 512], P(('qrow', 'kcol')), may hold values from -5 to 5
- code_rope: bfloat16 [16384, 64], P(('qrow', 'kcol')), may hold values from -6 to 6
- up_value: bfloat16 [128, 512, 128], P('kcol'), may hold values from -0.25 to 0.25
- out_weight: bfloat16 [16384, 5120], P('kcol', 'qrow'), may hold values from -0.046875 to 0.046875
Outputs:
- attended: bfloat16 [1024, 5120], P('kcol', 'qrow')
The draws below stay inside these ranges and needn't reach their ends.
All inputs are finite; a program needn't handle non-finite values.
Results may differ from the reference program's by a relative error of at most 0.012.
Values may be sent and summed in bfloat16 or wider, within the bound.
No kernel may reach another device: no remote copies, remote signals or barrier semaphores. Data moves between devices by JAX's collectives and lax.ppermute only.
A program may use at most 128 MiB of HBM per device.

```python
import math
import jax
import jax.numpy as jnp
from jax import lax

H = 128
LAT = 512
ROPE = 64
NOPE = 128
VD = 128
D = 5120
QB = 64
LQ = 1024
LK = 16384


def shared_codes(key):
    return jnp.clip(jax.random.normal(key, (LK, LAT), jnp.float32), -4.5, 4.5)


def draw_query_latent(key, part):
    base_codes = shared_codes(key)
    key = jax.random.fold_in(key, 7)
    latent = jnp.clip(1.5 * jax.random.normal(key, (LQ, H, LAT), jnp.float32), -9.0, 9.0)
    kinds = jax.random.randint(jax.random.fold_in(key, 11), (LQ, H), 0, 4)
    marked = jnp.arange(LQ) // QB % 4 == 1
    kinds = jnp.where(marked[:, None], kinds, 0)
    broad = jnp.clip(8.0 * jax.random.normal(jax.random.fold_in(key, 13), (LQ, H, LAT), jnp.float32), -36.0, 36.0)
    chosen = jax.random.randint(jax.random.fold_in(key, 17), (LQ, H), 0, LK - LQ + 1)
    matched = 8.0 * base_codes[chosen]
    latent = jnp.where((kinds == 2)[..., None], broad, latent)
    latent = jnp.where((kinds == 3)[..., None], matched, latent)
    latent = latent.reshape(LQ, H * LAT)
    return latent.astype(jnp.bfloat16)


def draw_code_latent(key, part):
    base_codes = shared_codes(key)
    return base_codes.astype(jnp.bfloat16)


def block_levels(rng, extent, cuts, low, largest):
    gain = 1.0
    for position, shards_of in cuts:
        heights = jax.random.uniform(jax.random.fold_in(jax.random.fold_in(rng, 6), position), (shards_of,), jnp.float32, low / len(cuts), largest / len(cuts))
        gain = gain * jnp.repeat(jnp.exp(heights), extent[position] // shards_of).reshape((-1,) + (1,) * (len(extent) - 1 - position))
    return gain


def gaussian(stream_key, dims, width, limit, cuts=(), kind=jnp.bfloat16):
    gain = block_levels(stream_key, dims, cuts, -0.22, 0.18) if cuts else 1.0
    result = jax.random.normal(stream_key, dims, jnp.float32) * width * gain
    return jnp.minimum(jnp.maximum(result, -limit), limit).astype(kind)


def setup_inputs(seed: int = 0) -> dict:
    keys = jax.random.split(jax.random.key(seed), 7)
    query_latent = draw_query_latent(jax.random.fold_in(keys[6], 71), 0)
    query_rope = gaussian(keys[1], (LQ, H * ROPE), 1.5, 6.0, ((0, 16), (1, 16)))
    code_latent = draw_code_latent(jax.random.fold_in(keys[6], 71), 0)
    code_rope = gaussian(keys[3], (LK, ROPE), 1.0, 6.0, ((0, 256),))
    up_value = gaussian(keys[4], (H, LAT, VD), LAT ** -0.5, 0.25, ((0, 16),))
    out_weight = gaussian(keys[5], (H * VD, D), (H * VD) ** -0.5, 0.046875, ((0, 16), (1, 16)))
    return {"query_latent": query_latent, "query_rope": query_rope, "code_latent": code_latent, "code_rope": code_rope, "up_value": up_value, "out_weight": out_weight}


def rotate(values, positions):
    half_width = values.shape[-1] // 2
    inverse = 10000.0 ** (-jnp.arange(half_width, dtype=jnp.float32) / half_width)
    angles = positions.astype(jnp.float32)[:, None] * inverse[None, :]
    cosine = jnp.cos(angles)
    sine_part = jnp.sin(angles)
    if values.ndim == 3:
        cosine = cosine[:, None, :]
        sine_part = sine_part[:, None, :]
    first_half = values[..., :half_width]
    second = values[..., half_width:]
    return jnp.concatenate([first_half * cosine - second * sine_part, second * cosine + first_half * sine_part], axis=-1)

def reference(query_latent, query_rope, code_latent, code_rope, up_value, out_weight):
    score_scale = 1.0 / math.sqrt(NOPE + ROPE)
    query_pos = LK - LQ + jnp.arange(LQ, dtype=jnp.int32)
    key_pos = jnp.arange(LK, dtype=jnp.int32)
    query_turned = rotate(query_rope.reshape(LQ, H, ROPE).astype(jnp.float32), query_pos).astype(jnp.bfloat16)
    key_turned = rotate(code_rope.astype(jnp.float32), key_pos).astype(jnp.bfloat16)
    visible = key_pos[None, :] <= query_pos[:, None]
    latent_heads = jnp.transpose(query_latent.reshape(LQ, H, LAT), (1, 0, 2))
    rope_heads = jnp.transpose(query_turned, (1, 0, 2))

    def one_head(members):
        query_lat, query_rot, value_map = members
        scores = jnp.dot(query_lat, code_latent.T, preferred_element_type=jnp.float32) + jnp.dot(query_rot, key_turned.T, preferred_element_type=jnp.float32)
        scores = jnp.where(visible, scores * score_scale, -1e+30)
        row_top = lax.optimization_barrier(jnp.max(scores, axis=1, keepdims=True))
        weights = jnp.exp(scores - row_top).astype(jnp.bfloat16)
        denominator = lax.optimization_barrier(jnp.sum(weights.astype(jnp.float32), axis=1, keepdims=True))
        numerator = jnp.dot(weights, code_latent, preferred_element_type=jnp.float32)
        latent_out = (numerator / denominator).astype(jnp.bfloat16)
        return jnp.dot(latent_out, value_map, preferred_element_type=jnp.float32).astype(jnp.bfloat16)
    head_out = lax.map(one_head, (latent_heads, rope_heads, up_value))
    flattened = jnp.transpose(head_out, (1, 0, 2)).reshape(LQ, H * VD)
    return jnp.dot(flattened, out_weight, preferred_element_type=jnp.float32).astype(jnp.bfloat16)
```

```python
import functools
import math

import jax
import jax.numpy as jnp
from jax import lax
from jax.experimental import pallas as pl
from jax.experimental.pallas import tpu as pltpu
from jax.sharding import Mesh, PartitionSpec as P

ROPE = 64
NOPE = 128
LAT = 512
VD = 128
HEADS = 8
QROWS = 64
WIDE = 640
SCALE = math.log2(math.e) / math.sqrt(NOPE + ROPE)
LOW = -1e30
VMEM = pl.BlockSpec(memory_space=pltpu.VMEM)
ANY = pl.BlockSpec(memory_space=pl.ANY)
BF = jnp.bfloat16
F32 = jnp.float32
X = ("xh", "xl")
SIZES = {"z": 8, "y": 4, X: 4, "core": 2, "xh": 2, "xl": 2}


def shift(value, axis, step):
    n = SIZES[axis]
    return lax.ppermute(value, axis, [(i, (i + step) % n) for i in range(n)])


def params(mib=48):
    return pltpu.CompilerParams(vmem_limit_bytes=mib * 2**20)


def table(first):
    half = ROPE // 2
    inverse = 10000.0 ** (-jnp.arange(half, dtype=F32) / half)
    angles = (first + jnp.arange(QROWS, dtype=jnp.int32)).astype(F32)[:, None] * inverse[None, :]
    return jnp.concatenate([jnp.cos(angles), jnp.sin(angles)], axis=1)


def turn(values, turns):
    half = ROPE // 2
    a, b = values[:, :half], values[:, half:]
    cosine, sine = turns[:, :half], turns[:, half:]
    return a * cosine - b * sine, b * cosine + a * sine


def key_kernel(first_ref, latent_ref, rope_ref, turns_ref, out_ref):
    out_ref[:, :LAT] = latent_ref[...]
    a, b = turn(rope_ref[...].astype(F32), turns_ref[...])
    lane = lax.broadcasted_iota(jnp.int32, (QROWS, ROPE), 1)
    pos = first_ref[0] + lax.broadcasted_iota(jnp.int32, (QROWS, ROPE), 0)
    marks = jnp.where(lane == 0, pos // 128, jnp.where(lane == 1, pos % 128, 0)).astype(F32)
    out_ref[:, LAT:] = jnp.concatenate([a, b, marks], axis=1).astype(BF)


def make_keys(first, latent, rope, turns):
    return pl.pallas_call(
        key_kernel,
        out_shape=jax.ShapeDtypeStruct((QROWS, WIDE), BF),
        in_specs=[pl.BlockSpec(memory_space=pltpu.SMEM), VMEM, VMEM, VMEM],
        out_specs=VMEM,
        compiler_params=params(),
    )(first, latent, rope, turns)


def query_kernel(own_ref, other_ref, own_rope_ref, other_rope_ref, turns_ref, out_ref):
    for side, (latent, rope) in enumerate(
        ((own_ref, own_rope_ref), (other_ref, other_rope_ref))
    ):
        for h in range(HEADS):
            rows = pl.ds((side * HEADS + h) * QROWS, QROWS)
            out_ref[rows, :LAT] = latent[:, h * LAT : (h + 1) * LAT]
            a, b = turn(rope[:, h * ROPE : (h + 1) * ROPE].astype(F32), turns_ref[...])
            rest = jnp.zeros((QROWS, WIDE - LAT - ROPE), F32)
            out_ref[rows, LAT:] = jnp.concatenate([a, b, rest], axis=1).astype(BF)


def make_queries(own, other, own_rope, other_rope, turns):
    return pl.pallas_call(
        query_kernel,
        out_shape=jax.ShapeDtypeStruct((2 * HEADS * QROWS, WIDE), BF),
        in_specs=[VMEM] * 5,
        out_specs=VMEM,
        compiler_params=params(),
    )(own, other, own_rope, other_rope, turns)


def attend_kernel(sizes, block, begin, first_ref, q_ref, *refs):
    count = len(sizes)
    pieces, refs = refs[:count], refs[count:]
    if begin:
        m_ref, l_ref, a_ref, keys, turned, bias, sems = refs
        m_ref[...] = jnp.full_like(m_ref, LOW)
        l_ref[...] = jnp.zeros_like(l_ref)
        a_ref[...] = jnp.zeros_like(a_ref)
    else:
        m_in, l_in, a_in, m_ref, l_ref, a_ref, keys, turned, bias, sems = refs
    offset = 0
    copies = []
    for i, size in enumerate(sizes):
        copy = pltpu.make_async_copy(pieces[i], keys.at[pl.ds(offset, size)], sems.at[i])
        copy.start()
        copies.append(copy)
        offset += size
    if not begin:
        m_ref[...] = m_in[...]
        l_ref[...] = l_in[...]
        a_ref[...] = a_in[...]
    for copy in copies:
        copy.wait()
    rows = q_ref.shape[0]
    step_rows = 256

    def one_block(index, carry):
        here = pl.ds(pl.multiple_of(index * block, block), block)
        turned[...] = keys[here, :].T
        marks = turned[LAT + ROPE : LAT + ROPE + 16, :].astype(F32)
        key_pos = marks[0:1, :] * 128.0 + marks[1:2, :]
        query_pos = (
            first_ref[0] + lax.broadcasted_iota(jnp.int32, (QROWS, block), 0)
        ).astype(F32)
        bias[...] = jnp.where(key_pos <= query_pos, 0.0, LOW)

        def score(i):
            s = jnp.dot(
                q_ref[i * step_rows : (i + 1) * step_rows, :],
                turned[...],
                preferred_element_type=F32,
            )
            s = s.reshape(step_rows // QROWS, QROWS, block) + bias[...][None]
            return s.reshape(step_rows, block)

        steps = rows // step_rows
        s = score(0)
        for i in range(steps):
            following = score(i + 1) if i + 1 < steps else None
            r = slice(i * step_rows, (i + 1) * step_rows)
            m_old = m_ref[r, :1]
            m_new = jnp.maximum(m_old, jnp.max(s, axis=1, keepdims=True))
            weights = jnp.exp2((s - m_new) * SCALE)
            fade = jnp.exp2((m_old - m_new) * SCALE)
            total = l_ref[r, :1] * fade + jnp.sum(weights, axis=1, keepdims=True)
            l_ref[r, :] = jnp.broadcast_to(total, (step_rows, 128))
            m_ref[r, :] = jnp.broadcast_to(m_new, (step_rows, 128))
            a_ref[r, :] = a_ref[r, :] * fade + jnp.dot(
                weights.astype(BF), keys[here, :LAT], preferred_element_type=F32
            )
            s = following
        return carry

    lax.fori_loop(0, offset // block, one_block, 0)


def attend(first, q, pieces, state, block):
    rows = q.shape[0]
    sizes = tuple(p.shape[0] for p in pieces)
    total = sum(sizes)
    assert total % block == 0
    begin = state is None
    shapes = [
        jax.ShapeDtypeStruct((rows, 128), F32),
        jax.ShapeDtypeStruct((rows, 128), F32),
        jax.ShapeDtypeStruct((rows, LAT), F32),
    ]
    return pl.pallas_call(
        functools.partial(attend_kernel, sizes, block, begin),
        out_shape=shapes,
        in_specs=[pl.BlockSpec(memory_space=pltpu.SMEM), VMEM]
        + [ANY] * len(sizes)
        + ([] if begin else [VMEM] * 3),
        out_specs=[VMEM] * 3,
        scratch_shapes=[
            pltpu.VMEM((total, WIDE), BF),
            pltpu.VMEM((WIDE, block), BF),
            pltpu.VMEM((QROWS, block), F32),
            pltpu.SemaphoreType.DMA((len(sizes),)),
        ],
        compiler_params=params(),
        cost_estimate=pl.CostEstimate(
            flops=2 * rows * total * (WIDE + LAT) * 3 // 2,
            bytes_accessed=2 * total * WIDE + 6 * 2**20,
            transcendentals=rows * total,
        ),
    )(first, q, *pieces, *(() if begin else state))


def project_kernel(m_ref, l_ref, a_ref, up_ref, other_up_ref, own_ref, other_ref, stat_ref, other_stat_ref):
    lane = lax.broadcasted_iota(jnp.int32, (QROWS, 128), 1)
    for side, (up, out, stat) in enumerate(
        ((up_ref, own_ref, stat_ref), (other_up_ref, other_ref, other_stat_ref))
    ):
        logs = jnp.zeros((QROWS, 128), F32)
        for h in range(HEADS):
            rows = pl.ds((side * HEADS + h) * QROWS, QROWS)
            l = l_ref[rows, :1]
            latent = (a_ref[rows, :] / l).astype(BF)
            value = jnp.dot(latent, up[h], preferred_element_type=F32)
            out[:, h * VD : (h + 1) * VD] = value.astype(out.dtype)
            logs = jnp.where(lane == h, m_ref[rows, :1] * SCALE + jnp.log2(l), logs)
        stat[...] = logs


def project(state, up, other_up):
    shape = (QROWS, HEADS * VD)
    return pl.pallas_call(
        project_kernel,
        out_shape=[
            jax.ShapeDtypeStruct(shape, F32),
            jax.ShapeDtypeStruct(shape, BF),
            jax.ShapeDtypeStruct((QROWS, 128), F32),
            jax.ShapeDtypeStruct((QROWS, 128), F32),
        ],
        in_specs=[VMEM] * 5,
        out_specs=[VMEM] * 4,
        compiler_params=params(),
    )(*state, up, other_up)


def merge_kernel(own_ref, other_ref, stat_ref, other_stat_ref, out_ref):
    gap = other_stat_ref[...] - stat_ref[...]
    own_share = 1.0 / (1.0 + jnp.exp2(gap))
    other_share = 1.0 / (1.0 + jnp.exp2(-gap))
    for h in range(HEADS):
        c = slice(h * VD, (h + 1) * VD)
        out_ref[:, c] = (
            own_ref[:, c] * own_share[:, h : h + 1]
            + other_ref[:, c].astype(F32) * other_share[:, h : h + 1]
        ).astype(BF)


def merge(own, other, stat, other_stat):
    return pl.pallas_call(
        merge_kernel,
        out_shape=jax.ShapeDtypeStruct(own.shape, BF),
        in_specs=[VMEM] * 4,
        out_specs=VMEM,
        compiler_params=params(),
    )(own, other, stat, other_stat)


def ring4(block, axis):
    half = block.shape[0] // 2
    plus, minus = shift(block, axis, 1), shift(block, axis, -1)
    far = [shift(plus[:half], axis, 1), shift(minus[half:], axis, -1)]
    return [plus, minus], far


def ring8(block):
    plus, minus, found = block, block, []
    for _ in range(3):
        plus, minus = shift(plus, "z", 1), shift(minus, "z", -1)
        found += [plus, minus]
    half = block.shape[0] // 2
    return found, [shift(plus[:half], "z", 1), shift(minus[half:], "z", -1)]


def local(query_latent, query_rope, code_latent, code_rope, up_value, out_weight):
    z, xh, y, xl, core = (lax.axis_index(a) for a in ("z", "xh", "y", "xl", "core"))
    row = z * 2 + xh
    col = (y * 2 + xl) * 2 + core
    key_first = (row * 16 + col) * QROWS
    query_first = 15360 + row * QROWS
    key_turns, query_turns = table(key_first), table(query_first)
    keys = make_keys(key_first.reshape(1).astype(jnp.int32), code_latent, code_rope, key_turns)
    first = query_first.reshape(1).astype(jnp.int32)

    other_latent = shift(query_latent, "core", 1)
    other_rope = shift(query_rope, "core", 1)
    q = make_queries(query_latent, other_latent, query_rope, other_rope, query_turns)

    part = keys[:16]
    line = jnp.concatenate([part] + [shift(part, X, s) for s in (1, -1, 2)], axis=0)
    plane = jnp.concatenate([line] + [shift(line, "y", s) for s in (1, -1, 2)], axis=0)
    near, far = ring8(keys[16:])
    cols = [keys[16:]] + near + [jnp.concatenate([far[0], far[1]], axis=0)]
    col_b = jnp.concatenate([c[:24] for c in cols], axis=0)
    col_c = jnp.concatenate([c[24:] for c in cols], axis=0)
    a_near, a_far = ring8(plane)
    near_b, far_b = ring4(col_b, "y")
    near_c, far_c = ring4(col_c, X)
    plane_b = jnp.concatenate([col_b] + near_b + far_b, axis=0)
    plane_c = jnp.concatenate([col_c] + near_c + far_c, axis=0)
    near_x, far_x = ring4(plane_b, X)
    near_y, far_y = ring4(plane_c, "y")

    other_up = shift(up_value, "core", 1)
    other_weight = shift(out_weight, "xh", 1)

    state = attend(first, q, [plane, col_b, col_c] + a_near[:2], None, 1152)
    state = attend(first, q, near_b + far_b + near_c + far_c, state, 1152)
    state = attend(first, q, a_near[2:], state, 1024)
    state = attend(first, q, near_x + near_y, state, 1024)
    state = attend(first, q, a_far + far_x + far_y, state, 896)

    own, other, stat, other_stat = project(state, up_value, other_up)
    got, got_stat = shift(other, "core", 1), shift(other_stat, "core", 1)
    heads = merge(own, got, stat, got_stat)

    near, far = ring8(heads)
    blocks = [heads, near[0], near[2], near[4], jnp.concatenate(far, axis=0), near[5], near[3], near[1]]
    found = jnp.concatenate(blocks, axis=0).reshape(8, QROWS, HEADS * VD)
    order = (z - jnp.arange(8)) % 8
    found = found[order].reshape(8 * QROWS, HEADS * VD)
    own_part = jnp.dot(found, out_weight, preferred_element_type=F32)
    other_part = jnp.dot(found, other_weight, preferred_element_type=F32)
    mine = xh == core
    keep = jnp.where(mine, own_part, other_part)
    give = jnp.where(mine, other_part, own_part).astype(BF)
    part = keep + shift(give, "core", 1).astype(F32)
    part = part.reshape(4, 2 * QROWS, out_weight.shape[1])
    sent = part.astype(BF)
    total = lax.dynamic_index_in_dim(part, y, 0, False)
    for s in (1, -1, 2):
        total = total + shift(
            lax.dynamic_index_in_dim(sent, (y + s) % 4, 0, False), "y", s
        ).astype(F32)
    total = total.astype(BF).reshape(2, QROWS, out_weight.shape[1])
    result = None
    for s in (0, 1):
        perm = []
        for a in range(2):
            for b in range(2):
                for c in range(2):
                    perm.append(((a * 2 + b) * 2 + c, (c * 2 + (b ^ s)) * 2 + a))
        got = lax.ppermute(
            lax.dynamic_index_in_dim(total, (xl + s) % 2, 0, False), ("xh", "xl", "core"), perm
        ).astype(F32)
        result = got if result is None else result + got
    return result.astype(BF)


def solution(mesh):
    fine = Mesh(mesh.devices.reshape(8, 2, 4, 2, 2), ("z", "xh", "y", "xl", "core"))
    row, col = ("z", "xh"), ("y", "xl", "core")
    in_specs = (P(row, col), P(row, col), P(row + col, None), P(row + col, None), P(col, None, None), P(col, row))
    return jax.shard_map(local, mesh=fine, in_specs=in_specs, out_specs=P(col, row), check_vma=False)
```

```python
import functools
import math

import jax
import jax.numpy as jnp
from jax import lax
from jax.experimental import pallas as pl
from jax.experimental.pallas import tpu as pltpu
from jax.sharding import Mesh, PartitionSpec as P

ROPE = 64
NOPE = 128
LAT = 512
VD = 128
HEADS = 8
QROWS = 64
WIDE = 640
SCALE = math.log2(math.e) / math.sqrt(NOPE + ROPE)
LOW = -1e30
VMEM = pl.BlockSpec(memory_space=pltpu.VMEM)
SMEM = pl.BlockSpec(memory_space=pltpu.SMEM)
ROWS = 2 * HEADS * QROWS
STEP = 256
BLOCK = 1024
BF = jnp.bfloat16
F32 = jnp.float32
AXES = ("z", "xh", "y", "xl", "core")


def flat(z, x, y, core):
    return (((z * 2 + x // 2) * 4 + y) * 2 + x % 2) * 2 + core


def move(value, target):
    perm = []
    for z in range(8):
        for x in range(4):
            for y in range(4):
                for core in range(2):
                    perm.append((flat(z, x, y, core), flat(*target(z, x, y, core))))
    return lax.ppermute(value, AXES, perm)


def to_core(z, x, y, core):
    return z, x, y, 1 - core


def to_pair(z, x, y, core):
    return z ^ 1, x, y, core


def along_z(step):
    return lambda z, x, y, core: ((z + step) % 8, x, y, core)


def along_y(step):
    return lambda z, x, y, core: (z, x, (y + step) % 4, core)


def along_x(step):
    return lambda z, x, y, core: (z, (x + step) % 4, y, core)


def along_first(step):
    return lambda z, x, y, core: (
        (z, (x + step) % 4, y, core) if core else (z, x, (y + step) % 4, core)
    )


def along_second(step):
    return lambda z, x, y, core: (
        (z, x, (y + step) % 4, core) if core else (z, (x + step) % 4, y, core)
    )


def params(mib=32):
    return pltpu.CompilerParams(vmem_limit_bytes=mib * 2**20)


def table(first):
    lane = jnp.arange(128, dtype=jnp.int32)
    half = ROPE // 2
    inverse = 10000.0 ** (-(lane % half).astype(F32) / half)
    angles = (first + jnp.arange(QROWS, dtype=jnp.int32)).astype(F32)[:, None] * inverse[None, :]
    sign = jnp.where(lane % ROPE < half, -1.0, 1.0)
    return jnp.cos(angles), jnp.sin(angles) * sign[None, :]


def key_kernel(first_ref, latent_ref, rope_ref, cos_ref, sin_ref, out_ref):
    half = ROPE // 2
    out_ref[:, :LAT] = latent_ref[...]
    values = rope_ref[...].astype(F32)
    a, b = values[:, :half], values[:, half:]
    cosine, sine = cos_ref[:, :half], sin_ref[:, half:ROPE]
    lane = lax.broadcasted_iota(jnp.int32, (QROWS, ROPE), 1)
    pos = first_ref[0] + lax.broadcasted_iota(jnp.int32, (QROWS, ROPE), 0)
    marks = jnp.where(lane == 0, pos // 128, jnp.where(lane == 1, pos % 128, 0)).astype(F32)
    out_ref[:, LAT:] = jnp.concatenate(
        [a * cosine - b * sine, b * cosine + a * sine, marks], axis=1
    ).astype(BF)


def make_keys(first, latent, rope, cosine, sine):
    return pl.pallas_call(
        key_kernel,
        out_shape=jax.ShapeDtypeStruct((QROWS, WIDE), BF),
        in_specs=[SMEM] + [VMEM] * 4,
        out_specs=VMEM,
        compiler_params=params(),
    )(first, latent, rope, cosine, sine)


def query_kernel(own_ref, other_ref, cos_ref, sin_ref, out_ref):
    lane = lax.broadcasted_iota(jnp.int32, (QROWS, 128), 1)
    for side, ref in enumerate((own_ref, other_ref)):
        for h in range(0, HEADS, 2):
            start = HEADS * LAT + h * ROPE
            pair = ref[:, start : start + 2 * ROPE].astype(F32)
            swapped = jnp.where(
                lane % ROPE < ROPE // 2, pltpu.roll(pair, 96, 1), pltpu.roll(pair, 32, 1)
            )
            turned = pair * cos_ref[...] + swapped * sin_ref[...]
            for k, value in enumerate((turned, pltpu.roll(turned, ROPE, 1))):
                rows = pl.ds((side * HEADS + h + k) * QROWS, QROWS)
                out_ref[rows, :LAT] = ref[:, (h + k) * LAT : (h + k + 1) * LAT]
                out_ref[rows, LAT:] = jnp.where(lane < ROPE, value, 0.0).astype(BF)


def make_queries(own, other, cosine, sine):
    return pl.pallas_call(
        query_kernel,
        out_shape=pltpu.VMEM((ROWS, WIDE), BF),
        in_specs=[VMEM] * 4,
        out_specs=VMEM,
        compiler_params=params(),
        cost_estimate=pl.CostEstimate(flops=10**9, bytes_accessed=2**22, transcendentals=0),
    )(own, other, cosine, sine)


def attend_kernel(count, groups, begin, *refs):
    firsts, refs = refs[:groups], refs[groups:]
    queries, refs = refs[:groups], refs[groups:]
    pieces, refs = refs[:count], refs[count:]
    if not begin:
        refs = refs[3 * groups :]
    states = [refs[3 * g : 3 * g + 3] for g in range(groups)]
    turned, bias, joined = refs[3 * groups :]
    if begin:
        for m_ref, l_ref, a_ref in states:
            m_ref[...] = jnp.full_like(m_ref, LOW)
            l_ref[...] = jnp.zeros_like(l_ref)
            a_ref[...] = jnp.zeros_like(a_ref)
    if pieces[0].shape[0] < BLOCK:
        step = pieces[0].shape[0]
        for i, piece in enumerate(pieces):
            joined[i * step : (i + 1) * step, :] = piece[...]
        pieces = [joined]
    offsets = lax.broadcasted_iota(jnp.int32, (QROWS, BLOCK), 0)
    for keys in pieces:
        turned[...] = keys[...].T
        marks = turned[LAT + ROPE : LAT + ROPE + 16, :].astype(F32)
        key_pos = marks[0:1, :] * 128.0 + marks[1:2, :]
        for g in range(groups):
            query_pos = (firsts[g][0] + offsets).astype(F32)
            bias[g] = jnp.where(key_pos <= query_pos, 0.0, LOW)
        work = [(g, i) for g in range(groups) for i in range(ROWS // STEP)]

        def score(item):
            g, i = item
            s = jnp.dot(
                queries[g][i * STEP : (i + 1) * STEP, :],
                turned[...],
                preferred_element_type=F32,
            )
            s = s.reshape(STEP // QROWS, QROWS, BLOCK) + bias[g][None]
            return s.reshape(STEP, BLOCK)

        s = score(work[0])
        for n, (g, i) in enumerate(work):
            following = score(work[n + 1]) if n + 1 < len(work) else None
            m_ref, l_ref, a_ref = states[g]
            r = slice(i * STEP, (i + 1) * STEP)
            m_old = m_ref[r, :1]
            m_new = jnp.maximum(m_old, jnp.max(s, axis=1, keepdims=True))
            weights = jnp.exp2((s - m_new) * SCALE)
            fade = jnp.exp2((m_old - m_new) * SCALE)
            total = l_ref[r, :1] * fade + jnp.sum(weights, axis=1, keepdims=True)
            l_ref[r, :] = jnp.broadcast_to(total, (STEP, 128))
            m_ref[r, :] = jnp.broadcast_to(m_new, (STEP, 128))
            a_ref[r, :] = a_ref[r, :] * fade + jnp.dot(
                weights.astype(BF), keys[:, :LAT], preferred_element_type=F32
            )
            s = following


def attend(firsts, queries, pieces, states):
    groups = len(queries)
    begin = states is None
    total = sum(p.shape[0] for p in pieces)
    shapes = [
        pltpu.VMEM((ROWS, 128), F32),
        pltpu.VMEM((ROWS, 128), F32),
        pltpu.VMEM((ROWS, LAT), F32),
    ] * groups
    flat_states = [] if begin else [v for state in states for v in state]
    before = 2 * groups + len(pieces)
    out = pl.pallas_call(
        functools.partial(attend_kernel, len(pieces), groups, begin),
        out_shape=shapes,
        in_specs=[SMEM] * groups + [VMEM] * (groups + len(pieces) + len(flat_states)),
        out_specs=[VMEM] * (3 * groups),
        input_output_aliases={before + i: i for i in range(len(flat_states))},
        scratch_shapes=[
            pltpu.VMEM((WIDE, BLOCK), BF),
            pltpu.VMEM((groups, QROWS, BLOCK), F32),
            pltpu.VMEM((BLOCK, WIDE), BF),
        ],
        compiler_params=params(),
        cost_estimate=pl.CostEstimate(
            flops=2 * groups * ROWS * total * (WIDE + LAT) * 3 // 2,
            bytes_accessed=2 * total * WIDE,
            transcendentals=groups * ROWS * total,
        ),
    )(*firsts, *queries, *pieces, *flat_states)
    return [tuple(out[3 * g : 3 * g + 3]) for g in range(groups)]


def pack_logs(logs):
    high = logs.astype(BF)
    left = logs - high.astype(F32)
    middle = left.astype(BF)
    low = (left - middle.astype(F32)).astype(BF)
    parts = [p.astype(F32)[:, :HEADS] for p in (high, middle, low)]
    rest = jnp.zeros((logs.shape[0], 128 - 3 * HEADS), F32)
    return jnp.concatenate(parts + [rest], axis=1).astype(BF)


def unpack_logs(packed):
    packed = packed.astype(F32)
    high, middle, low = (packed[:, i * HEADS : (i + 1) * HEADS] for i in range(3))
    return high + middle + low


WIDTH = HEADS * VD


def project_kernel(m_ref, l_ref, a_ref, up_ref, other_up_ref, own_ref, stat_ref, other_ref):
    lane = lax.broadcasted_iota(jnp.int32, (QROWS, 128), 1)
    for side, (up, out) in enumerate(((up_ref, own_ref), (other_up_ref, other_ref))):
        logs = jnp.zeros((QROWS, 128), F32)
        for h in range(HEADS):
            rows = pl.ds((side * HEADS + h) * QROWS, QROWS)
            l = l_ref[rows, :1]
            latent = (a_ref[rows, :] / l).astype(BF)
            value = jnp.dot(latent, up[h], preferred_element_type=F32)
            out[:, h * VD : (h + 1) * VD] = value.astype(out.dtype)
            logs = jnp.where(lane == h, m_ref[rows, :1] * SCALE + jnp.log2(l), logs)
        if side:
            other_ref[:, WIDTH:] = pack_logs(logs)
        else:
            stat_ref[...] = logs


def project(state, up, other_up):
    return pl.pallas_call(
        project_kernel,
        out_shape=[
            jax.ShapeDtypeStruct((QROWS, WIDTH), F32),
            jax.ShapeDtypeStruct((QROWS, 128), F32),
            jax.ShapeDtypeStruct((QROWS, WIDTH + 128), BF),
        ],
        in_specs=[VMEM] * 5,
        out_specs=[VMEM] * 3,
        compiler_params=params(),
    )(*state, up, other_up)


def merge_kernel(keep_logs, own_ref, stat_ref, *refs):
    others, out_ref = refs[:-1], refs[-1]
    logs = [stat_ref[:, :HEADS]] + [unpack_logs(o[:, WIDTH:]) for o in others]
    top = functools.reduce(jnp.maximum, logs)
    shares = [jnp.exp2(v - top) for v in logs]
    total = functools.reduce(lambda a, b: a + b, shares)
    shares = [s / total for s in shares]
    for h in range(HEADS):
        c = slice(h * VD, (h + 1) * VD)
        value = own_ref[:, c] * shares[0][:, h : h + 1]
        for other, share in zip(others, shares[1:]):
            value = value + other[:, c].astype(F32) * share[:, h : h + 1]
        out_ref[:, c] = value.astype(BF)
    if keep_logs:
        joint = top + jnp.log2(total)
        rest = jnp.zeros((QROWS, 128 - HEADS), F32)
        out_ref[:, WIDTH:] = pack_logs(jnp.concatenate([joint, rest], axis=1))


def merge(keep_logs, own, stat, *others):
    return pl.pallas_call(
        functools.partial(merge_kernel, keep_logs),
        out_shape=jax.ShapeDtypeStruct((QROWS, WIDTH + (128 if keep_logs else 0)), BF),
        in_specs=[VMEM] * (2 + len(others)),
        out_specs=VMEM,
        compiler_params=params(),
    )(own, stat, *others)


def local(query_latent, query_rope, code_latent, code_rope, up_value, out_weight):
    z, xh, y, xl, core = (lax.axis_index(a) for a in AXES)
    row = z * 2 + xh
    pair_row = (z ^ 1) * 2 + xh
    col = (y * 2 + xl) * 2 + core
    key_first = (row * 16 + col) * QROWS
    query_first = 15360 + row * QROWS
    pair_first = 15360 + pair_row * QROWS
    key_first = key_first.reshape(1).astype(jnp.int32)
    first = query_first.reshape(1).astype(jnp.int32)
    second = pair_first.reshape(1).astype(jnp.int32)
    keys = make_keys(key_first, code_latent, code_rope, *table(key_first))
    column = jnp.concatenate([keys] + [move(keys, along_z(s)) for s in (4, 2, -2)], axis=0)

    queries = jnp.concatenate([query_latent, query_rope], axis=1)
    core_queries = move(queries, to_core)
    pair_queries = move(queries, to_pair)
    q1 = make_queries(queries, core_queries, *table(first))

    plane = jnp.concatenate([column] + [move(column, along_first(s)) for s in (2, 1, -1)], axis=0)
    plane, q1, pair_queries = lax.optimization_barrier((plane, q1, pair_queries))
    plus, minus = move(plane, along_second(1)), move(plane, along_second(-1))
    far = [move(plus[:512], along_second(1)), move(minus[512:], along_second(-1))]
    both_queries = move(pair_queries, to_core)
    other_up = move(up_value, to_core)
    pair_weight = move(out_weight, to_pair)
    q2 = make_queries(pair_queries, both_queries, *table(second))

    (s1,) = attend([first], [q1], [plane], None)
    (s2,) = attend([second], [q2], [plane], None)
    s1, s2 = attend([first, second], [q1, q2], [plus], [s1, s2])
    (s2,) = attend([second], [q2], [minus], [s2])
    pair_weight, *far = lax.optimization_barrier((pair_weight, *far))
    side_weights = move(jnp.concatenate([out_weight, pair_weight], axis=0), along_x(2))
    (s2,) = attend([second], [q2], far, [s2])
    own2, stat2, other2 = project(s2, up_value, other_up)
    s1, own2 = lax.optimization_barrier((s1, own2))
    (s1,) = attend([first], [q1], [minus], [s1])
    sent2 = merge(True, own2, stat2, move(other2, to_core))
    sent2, s1 = lax.optimization_barrier((sent2, s1))
    (s1,) = attend([first], [q1], far, [s1])
    own1, stat1, other1 = project(s1, up_value, other_up)
    heads = merge(False, own1, stat1, move(other1, to_core), move(sent2, to_pair))

    blocks = [heads, move(heads, along_z(2)), move(heads, along_z(4)), move(heads, along_z(-2))]
    found = jnp.concatenate(blocks, axis=0)
    same = xh == core
    sides = (side_weights[: HEADS * VD], side_weights[HEADS * VD :])
    keep_w = [jnp.where(same, o, s) for o, s in zip((out_weight, pair_weight), sides)]
    give_w = [jnp.where(same, s, o) for o, s in zip((out_weight, pair_weight), sides)]
    found, keep_w, give_w = lax.optimization_barrier((found, keep_w, give_w))
    give = jnp.stack([jnp.dot(found, w, preferred_element_type=F32).astype(BF) for w in give_w])
    keep = jnp.stack([jnp.dot(found, w, preferred_element_type=F32) for w in keep_w])
    columns = out_weight.shape[1]
    part = (keep + move(give, to_core).astype(F32)).reshape(2, 4, QROWS, columns)
    sent = part.astype(BF)
    total = None
    for dy in (2, 1, 3, 0):
        block = (z // 2 - (y + dy)) % 4
        if dy:
            got = move(lax.dynamic_index_in_dim(sent, block, 1, False), along_y(dy)).astype(F32)
        else:
            got = lax.dynamic_index_in_dim(part, block, 1, False)
        total = got if total is None else total + got
    total = total.astype(BF)
    result = None
    for s in (0, 1):

        def target(z, x, y, core):
            return (z & 6) | ((x & 1) ^ s), core * 2 + (z & 1), y, x >> 1

        piece = lax.dynamic_index_in_dim(total, (xl ^ s) ^ (z & 1), 0, False)
        got = move(piece, target).astype(F32)
        result = got if result is None else result + got
    return result.astype(BF)


def solution(mesh):
    fine = Mesh(mesh.devices.reshape(8, 2, 4, 2, 2), AXES)
    row, col = ("z", "xh"), ("y", "xl", "core")
    in_specs = (P(row, col), P(row, col), P(row + col, None), P(row + col, None), P(col, None, None), P(col, row))
    return jax.shard_map(local, mesh=fine, in_specs=in_specs, out_specs=P(col, row), check_vma=False)
```

```python
import functools
import math

import jax
import jax.numpy as jnp
from jax import lax
from jax.experimental import pallas as pl
from jax.experimental.pallas import tpu as pltpu
from jax.sharding import Mesh, PartitionSpec as P

ROPE = 64
NOPE = 128
LAT = 512
VD = 128
HEADS = 8
QROWS = 64
WIDE = 640
SCALE = math.log2(math.e) / math.sqrt(NOPE + ROPE)
LOW = -1e30
VMEM = pl.BlockSpec(memory_space=pltpu.VMEM)
SMEM = pl.BlockSpec(memory_space=pltpu.SMEM)
ROWS = 2 * HEADS * QROWS
STEP = 256
BLOCK = 1024
BF = jnp.bfloat16
F32 = jnp.float32
AXES = ("z", "xh", "y", "xl", "core")


def flat(z, x, y, core):
    return (((z * 2 + x // 2) * 4 + y) * 2 + x % 2) * 2 + core


def move(value, target):
    perm = []
    for z in range(8):
        for x in range(4):
            for y in range(4):
                for core in range(2):
                    perm.append((flat(z, x, y, core), flat(*target(z, x, y, core))))
    return lax.ppermute(value, AXES, perm)


def to_core(z, x, y, core):
    return z, x, y, 1 - core


def to_pair(z, x, y, core):
    return z ^ 1, x, y, core


def to_pair_core(z, x, y, core):
    return z ^ 1, x, y, 1 - core


def along_z(step):
    return lambda z, x, y, core: ((z + step) % 8, x, y, core)


def along_y(step):
    return lambda z, x, y, core: (z, x, (y + step) % 4, core)


def along_x(step):
    return lambda z, x, y, core: (z, (x + step) % 4, y, core)


def along_first(step):
    return lambda z, x, y, core: (
        (z, (x + step) % 4, y, core) if core else (z, x, (y + step) % 4, core)
    )


def along_second(step):
    return lambda z, x, y, core: (
        (z, x, (y + step) % 4, core) if core else (z, (x + step) % 4, y, core)
    )


def params(mib=32):
    return pltpu.CompilerParams(vmem_limit_bytes=mib * 2**20)


def table(first):
    lane = jnp.arange(128, dtype=jnp.int32)
    half = ROPE // 2
    inverse = 10000.0 ** (-(lane % half).astype(F32) / half)
    angles = (first + jnp.arange(QROWS, dtype=jnp.int32)).astype(F32)[:, None] * inverse[None, :]
    sign = jnp.where(lane % ROPE < half, -1.0, 1.0)
    return jnp.cos(angles), jnp.sin(angles) * sign[None, :]


def key_kernel(first_ref, latent_ref, rope_ref, cos_ref, sin_ref, out_ref):
    half = ROPE // 2
    out_ref[:, :LAT] = latent_ref[...]
    values = rope_ref[...].astype(F32)
    a, b = values[:, :half], values[:, half:]
    cosine, sine = cos_ref[:, :half], sin_ref[:, half:ROPE]
    lane = lax.broadcasted_iota(jnp.int32, (QROWS, ROPE), 1)
    pos = first_ref[0] + lax.broadcasted_iota(jnp.int32, (QROWS, ROPE), 0)
    marks = jnp.where(lane == 0, pos // 128, jnp.where(lane == 1, pos % 128, 0)).astype(F32)
    out_ref[:, LAT:] = jnp.concatenate(
        [a * cosine - b * sine, b * cosine + a * sine, marks], axis=1
    ).astype(BF)


def make_keys(first, latent, rope, cosine, sine):
    return pl.pallas_call(
        key_kernel,
        out_shape=jax.ShapeDtypeStruct((QROWS, WIDE), BF),
        in_specs=[SMEM] + [VMEM] * 4,
        out_specs=VMEM,
        compiler_params=params(),
    )(first, latent, rope, cosine, sine)


def query_kernel(own_ref, other_ref, cos_ref, sin_ref, out_ref):
    lane = lax.broadcasted_iota(jnp.int32, (QROWS, 128), 1)
    for side, ref in enumerate((own_ref, other_ref)):
        for h in range(0, HEADS, 2):
            start = HEADS * LAT + h * ROPE
            pair = ref[:, start : start + 2 * ROPE].astype(F32)
            swapped = jnp.where(
                lane % ROPE < ROPE // 2, pltpu.roll(pair, 96, 1), pltpu.roll(pair, 32, 1)
            )
            turned = pair * cos_ref[...] + swapped * sin_ref[...]
            for k, value in enumerate((turned, pltpu.roll(turned, ROPE, 1))):
                rows = pl.ds((side * HEADS + h + k) * QROWS, QROWS)
                out_ref[rows, :LAT] = ref[:, (h + k) * LAT : (h + k + 1) * LAT]
                out_ref[rows, LAT:] = jnp.where(lane < ROPE, value, 0.0).astype(BF)


def make_queries(own, other, cosine, sine):
    return pl.pallas_call(
        query_kernel,
        out_shape=pltpu.VMEM((ROWS, WIDE), BF),
        in_specs=[VMEM] * 4,
        out_specs=VMEM,
        compiler_params=params(),
        cost_estimate=pl.CostEstimate(flops=10**9, bytes_accessed=2**22, transcendentals=0),
    )(own, other, cosine, sine)


def attend_kernel(count, groups, begin, *refs):
    firsts, refs = refs[:groups], refs[groups:]
    queries, refs = refs[:groups], refs[groups:]
    pieces, refs = refs[:count], refs[count:]
    if not begin:
        refs = refs[3 * groups :]
    states = [refs[3 * g : 3 * g + 3] for g in range(groups)]
    turned, bias, joined = refs[3 * groups :]
    if begin:
        for m_ref, l_ref, a_ref in states:
            m_ref[...] = jnp.full_like(m_ref, LOW)
            l_ref[...] = jnp.zeros_like(l_ref)
            a_ref[...] = jnp.zeros_like(a_ref)
    blocks = [p for p in pieces if p.shape[0] == BLOCK]
    filled = 0
    for piece in pieces:
        step = piece.shape[0]
        if step < BLOCK:
            joined[filled : filled + step, :] = piece[...]
            filled += step
            if filled % BLOCK == 0:
                blocks.append(joined.at[filled - BLOCK : filled])
    offsets = lax.broadcasted_iota(jnp.int32, (QROWS, BLOCK), 0)
    for keys in blocks:
        turned[...] = keys[...].T
        marks = turned[LAT + ROPE : LAT + ROPE + 16, :].astype(F32)
        key_pos = marks[0:1, :] * 128.0 + marks[1:2, :]
        for g in range(groups):
            query_pos = (firsts[g][0] + offsets).astype(F32)
            bias[g] = jnp.where(key_pos <= query_pos, 0.0, LOW)
        work = [(g, i) for g in range(groups) for i in range(ROWS // STEP)]

        def score(item):
            g, i = item
            s = jnp.dot(
                queries[g][i * STEP : (i + 1) * STEP, :],
                turned[...],
                preferred_element_type=F32,
            )
            s = s.reshape(STEP // QROWS, QROWS, BLOCK) + bias[g][None]
            return s.reshape(STEP, BLOCK)

        s = score(work[0])
        for n, (g, i) in enumerate(work):
            following = score(work[n + 1]) if n + 1 < len(work) else None
            m_ref, l_ref, a_ref = states[g]
            r = slice(i * STEP, (i + 1) * STEP)
            m_old = m_ref[r, :1]
            m_new = jnp.maximum(m_old, jnp.max(s, axis=1, keepdims=True))
            weights = jnp.exp2((s - m_new) * SCALE)
            fade = jnp.exp2((m_old - m_new) * SCALE)
            total = l_ref[r, :1] * fade + jnp.sum(weights, axis=1, keepdims=True)
            l_ref[r, :] = jnp.broadcast_to(total, (STEP, 128))
            m_ref[r, :] = jnp.broadcast_to(m_new, (STEP, 128))
            a_ref[r, :] = a_ref[r, :] * fade + jnp.dot(
                weights.astype(BF), keys[:, :LAT], preferred_element_type=F32
            )
            s = following


def attend(firsts, queries, pieces, states):
    groups = len(queries)
    begin = states is None
    total = sum(p.shape[0] for p in pieces)
    shapes = [
        pltpu.VMEM((ROWS, 128), F32),
        pltpu.VMEM((ROWS, 128), F32),
        pltpu.VMEM((ROWS, LAT), F32),
    ] * groups
    flat_states = [] if begin else [v for state in states for v in state]
    before = 2 * groups + len(pieces)
    out = pl.pallas_call(
        functools.partial(attend_kernel, len(pieces), groups, begin),
        out_shape=shapes,
        in_specs=[SMEM] * groups + [VMEM] * (groups + len(pieces) + len(flat_states)),
        out_specs=[VMEM] * (3 * groups),
        input_output_aliases={before + i: i for i in range(len(flat_states))},
        scratch_shapes=[
            pltpu.VMEM((WIDE, BLOCK), BF),
            pltpu.VMEM((groups, QROWS, BLOCK), F32),
            pltpu.VMEM((max(total, BLOCK), WIDE), BF),
        ],
        compiler_params=params(),
        cost_estimate=pl.CostEstimate(
            flops=2 * groups * ROWS * total * (WIDE + LAT) * 3 // (2 * 2),
            bytes_accessed=2 * total * WIDE // 2,
            transcendentals=0,
        ),
    )(*firsts, *queries, *pieces, *flat_states)
    return [tuple(out[3 * g : 3 * g + 3]) for g in range(groups)]


def pack_logs(logs):
    high = logs.astype(BF)
    left = logs - high.astype(F32)
    middle = left.astype(BF)
    low = (left - middle.astype(F32)).astype(BF)
    parts = [p.astype(F32)[:, :HEADS] for p in (high, middle, low)]
    rest = jnp.zeros((logs.shape[0], 128 - 3 * HEADS), F32)
    return jnp.concatenate(parts + [rest], axis=1).astype(BF)


def unpack_logs(packed):
    packed = packed.astype(F32)
    high, middle, low = (packed[:, i * HEADS : (i + 1) * HEADS] for i in range(3))
    return high + middle + low


WIDTH = HEADS * VD


def project_kernel(keep, m_ref, l_ref, a_ref, up_ref, other_up_ref, own_ref, other_ref, *stat):
    lane = lax.broadcasted_iota(jnp.int32, (QROWS, 128), 1)
    for side, (up, out) in enumerate(((up_ref, own_ref), (other_up_ref, other_ref))):
        logs = jnp.zeros((QROWS, 128), F32)
        for h in range(HEADS):
            rows = pl.ds((side * HEADS + h) * QROWS, QROWS)
            l = l_ref[rows, :1]
            latent = (a_ref[rows, :] / l).astype(BF)
            value = jnp.dot(latent, up[h], preferred_element_type=F32)
            out[:, h * VD : (h + 1) * VD] = value.astype(out.dtype)
            logs = jnp.where(lane == h, m_ref[rows, :1] * SCALE + jnp.log2(l), logs)
        if keep and not side:
            stat[0][...] = logs
        else:
            out[:, WIDTH:] = pack_logs(logs)


def project(keep, state, up, other_up):
    packed = jax.ShapeDtypeStruct((QROWS, WIDTH + 128), BF)
    shapes = [packed, packed]
    if keep:
        shapes = [
            jax.ShapeDtypeStruct((QROWS, WIDTH), F32),
            packed,
            jax.ShapeDtypeStruct((QROWS, 128), F32),
        ]
    return pl.pallas_call(
        functools.partial(project_kernel, keep),
        out_shape=shapes,
        in_specs=[VMEM] * 5,
        out_specs=[VMEM] * len(shapes),
        compiler_params=params(),
    )(*state, up, other_up)


def merge_kernel(own_ref, stat_ref, *refs):
    others, out_ref = refs[:-1], refs[-1]
    logs = [stat_ref[:, :HEADS]] + [unpack_logs(o[:, WIDTH:]) for o in others]
    top = functools.reduce(jnp.maximum, logs)
    shares = [jnp.exp2(v - top) for v in logs]
    total = functools.reduce(lambda a, b: a + b, shares)
    shares = [s / total for s in shares]
    for h in range(HEADS):
        c = slice(h * VD, (h + 1) * VD)
        value = own_ref[:, c] * shares[0][:, h : h + 1]
        for other, share in zip(others, shares[1:]):
            value = value + other[:, c].astype(F32) * share[:, h : h + 1]
        out_ref[:, c] = value.astype(BF)


def merge(own, stat, *others):
    return pl.pallas_call(
        merge_kernel,
        out_shape=jax.ShapeDtypeStruct((QROWS, WIDTH), BF),
        in_specs=[VMEM] * (2 + len(others)),
        out_specs=VMEM,
        compiler_params=params(),
    )(own, stat, *others)


def local(query_latent, query_rope, code_latent, code_rope, up_value, out_weight):
    z, xh, y, xl, core = (lax.axis_index(a) for a in AXES)
    row = z * 2 + xh
    pair_row = (z ^ 1) * 2 + xh
    col = (y * 2 + xl) * 2 + core
    key_first = (row * 16 + col) * QROWS
    query_first = 15360 + row * QROWS
    pair_first = 15360 + pair_row * QROWS
    key_first = key_first.reshape(1).astype(jnp.int32)
    first = query_first.reshape(1).astype(jnp.int32)
    second = pair_first.reshape(1).astype(jnp.int32)
    keys = make_keys(key_first, code_latent, code_rope, *table(key_first))
    column = jnp.concatenate([keys] + [move(keys, along_z(s)) for s in (4, 2, -2)], axis=0)

    queries = jnp.concatenate([query_latent, query_rope], axis=1)
    core_queries = move(queries, to_core)
    pair_queries = move(queries, to_pair)
    q1 = make_queries(queries, core_queries, *table(first))

    plane = jnp.concatenate([column] + [move(column, along_first(s)) for s in (2, 1, -1)], axis=0)
    plane, q1, pair_queries = lax.optimization_barrier((plane, q1, pair_queries))
    low, high = plane[: BLOCK // 2], plane[BLOCK // 2 :]
    early = [move(low, along_second(1)), move(high, along_second(-1))]
    late = [move(high, along_second(1)), move(low, along_second(-1))]
    far = [move(early[0], along_second(1)), move(early[1], along_second(-1))]
    both_queries = move(pair_queries, to_core)
    other_up = move(up_value, to_core)
    pair_weight = move(out_weight, to_pair)
    q2 = make_queries(pair_queries, both_queries, *table(second))

    (s1,) = attend([first], [q1], [plane], None)
    (s2,) = attend([second], [q2], [plane], None)
    s1, s2 = attend([first, second], [q1, q2], early, [s1, s2])
    (s2,) = attend([second], [q2], late, [s2])
    pair_weight, s2, *far = lax.optimization_barrier((pair_weight, s2, *far))
    side_weights = move(jnp.concatenate([out_weight, pair_weight], axis=0), along_x(2))
    (s2,) = attend([second], [q2], far, [s2])
    own2, other2 = project(False, s2, up_value, other_up)
    s1, own2, other2 = lax.optimization_barrier((s1, own2, other2))
    (s1,) = attend([first], [q1], [*late, *far], [s1])
    s1, *sent = lax.optimization_barrier((s1, move(own2, to_pair), move(other2, to_pair_core)))
    own1, other1, stat1 = project(True, s1, up_value, other_up)
    heads = merge(own1, stat1, move(other1, to_core), *sent)

    blocks = [heads, move(heads, along_z(2)), move(heads, along_z(4)), move(heads, along_z(-2))]
    same = xh == core
    sides = (side_weights[: HEADS * VD], side_weights[HEADS * VD :])
    keep_w = [jnp.where(same, o, s) for o, s in zip((out_weight, pair_weight), sides)]
    give_w = [jnp.where(same, s, o) for o, s in zip((out_weight, pair_weight), sides)]
    blocks[1], keep_w, give_w = lax.optimization_barrier((blocks[1], keep_w, give_w))
    found = jnp.concatenate(blocks, axis=0)
    give = jnp.stack([jnp.dot(found, w, preferred_element_type=F32).astype(BF) for w in give_w])
    keep = jnp.stack([jnp.dot(found, w, preferred_element_type=F32) for w in keep_w])
    columns = out_weight.shape[1]
    part = (keep + move(give, to_core).astype(F32)).reshape(2, 4, QROWS, columns)
    sent = part.astype(BF)
    total = None
    for dy in (2, 1, 3, 0):
        block = (z // 2 - (y + dy)) % 4
        if dy:
            got = move(lax.dynamic_index_in_dim(sent, block, 1, False), along_y(dy)).astype(F32)
        else:
            got = lax.dynamic_index_in_dim(part, block, 1, False)
        total = got if total is None else total + got
    total = total.astype(BF)
    result = None
    for s in (0, 1):

        def target(z, x, y, core):
            return (z & 6) | ((x & 1) ^ s), core * 2 + (z & 1), y, x >> 1

        piece = lax.dynamic_index_in_dim(total, (xl ^ s) ^ (z & 1), 0, False)
        got = move(piece, target).astype(F32)
        result = got if result is None else result + got
    return result.astype(BF)


def solution(mesh):
    fine = Mesh(mesh.devices.reshape(8, 2, 4, 2, 2), AXES)
    row, col = ("z", "xh"), ("y", "xl", "core")
    in_specs = (P(row, col), P(row, col), P(row + col, None), P(row + col, None), P(col, None, None), P(col, row))
    return jax.shard_map(local, mesh=fine, in_specs=in_specs, out_specs=P(col, row), check_vma=False)
```

```python
import functools
import math

import jax
import jax.numpy as jnp
from jax import lax
from jax.experimental import pallas as pl
from jax.experimental.pallas import tpu as pltpu
from jax.sharding import Mesh, PartitionSpec as P

ROPE = 64
NOPE = 128
LAT = 512
VD = 128
HEADS = 8
QROWS = 64
WIDE = 640
SCALE = math.log2(math.e) / math.sqrt(NOPE + ROPE)
LOW = -1e30
VMEM = pl.BlockSpec(memory_space=pltpu.VMEM)
SMEM = pl.BlockSpec(memory_space=pltpu.SMEM)
ROWS = 2 * HEADS * QROWS
STEP = 256
BLOCK = 1024
BF = jnp.bfloat16
F32 = jnp.float32
AXES = ("z", "xh", "y", "xl", "core")


def flat(z, x, y, core):
    return (((z * 2 + x // 2) * 4 + y) * 2 + x % 2) * 2 + core


def move(value, target):
    perm = []
    for z in range(8):
        for x in range(4):
            for y in range(4):
                for core in range(2):
                    perm.append((flat(z, x, y, core), flat(*target(z, x, y, core))))
    return lax.ppermute(value, AXES, perm)


def to_core(z, x, y, core):
    return z, x, y, 1 - core


def to_pair(z, x, y, core):
    return z ^ 1, x, y, core


def to_pair_core(z, x, y, core):
    return z ^ 1, x, y, 1 - core


def along_z(step):
    return lambda z, x, y, core: ((z + step) % 8, x, y, core)


def along_y(step):
    return lambda z, x, y, core: (z, x, (y + step) % 4, core)


def along_x(step):
    return lambda z, x, y, core: (z, (x + step) % 4, y, core)


def along_first(step):
    return lambda z, x, y, core: (
        (z, (x + step) % 4, y, core) if core else (z, x, (y + step) % 4, core)
    )


def along_second(step):
    return lambda z, x, y, core: (
        (z, x, (y + step) % 4, core) if core else (z, (x + step) % 4, y, core)
    )


def params(mib=32):
    return pltpu.CompilerParams(vmem_limit_bytes=mib * 2**20)


def table(first):
    lane = jnp.arange(128, dtype=jnp.int32)
    half = ROPE // 2
    inverse = 10000.0 ** (-(lane % half).astype(F32) / half)
    angles = (first + jnp.arange(QROWS, dtype=jnp.int32)).astype(F32)[:, None] * inverse[None, :]
    sign = jnp.where(lane % ROPE < half, -1.0, 1.0)
    return jnp.cos(angles), jnp.sin(angles) * sign[None, :]


def key_kernel(first_ref, latent_ref, rope_ref, cos_ref, sin_ref, out_ref):
    half = ROPE // 2
    out_ref[:, :LAT] = latent_ref[...]
    values = rope_ref[...].astype(F32)
    a, b = values[:, :half], values[:, half:]
    cosine, sine = cos_ref[:, :half], sin_ref[:, half:ROPE]
    lane = lax.broadcasted_iota(jnp.int32, (QROWS, ROPE), 1)
    pos = first_ref[0] + lax.broadcasted_iota(jnp.int32, (QROWS, ROPE), 0)
    marks = jnp.where(lane == 0, pos // 128, jnp.where(lane == 1, pos % 128, 0)).astype(F32)
    out_ref[:, LAT:] = jnp.concatenate(
        [a * cosine - b * sine, b * cosine + a * sine, marks], axis=1
    ).astype(BF)


def make_keys(first, latent, rope, cosine, sine):
    return pl.pallas_call(
        key_kernel,
        out_shape=jax.ShapeDtypeStruct((QROWS, WIDE), BF),
        in_specs=[SMEM] + [VMEM] * 4,
        out_specs=VMEM,
        compiler_params=params(),
    )(first, latent, rope, cosine, sine)


def query_kernel(own_ref, other_ref, cos_ref, sin_ref, out_ref):
    lane = lax.broadcasted_iota(jnp.int32, (QROWS, 128), 1)
    for side, ref in enumerate((own_ref, other_ref)):
        for h in range(0, HEADS, 2):
            start = HEADS * LAT + h * ROPE
            pair = ref[:, start : start + 2 * ROPE].astype(F32)
            swapped = jnp.where(
                lane % ROPE < ROPE // 2, pltpu.roll(pair, 96, 1), pltpu.roll(pair, 32, 1)
            )
            turned = pair * cos_ref[...] + swapped * sin_ref[...]
            for k, value in enumerate((turned, pltpu.roll(turned, ROPE, 1))):
                rows = pl.ds((side * HEADS + h + k) * QROWS, QROWS)
                out_ref[rows, :LAT] = ref[:, (h + k) * LAT : (h + k + 1) * LAT]
                out_ref[rows, LAT:] = jnp.where(lane < ROPE, value, 0.0).astype(BF)


def make_queries(own, other, cosine, sine):
    return pl.pallas_call(
        query_kernel,
        out_shape=pltpu.VMEM((ROWS, WIDE), BF),
        in_specs=[VMEM] * 4,
        out_specs=VMEM,
        compiler_params=params(),
        cost_estimate=pl.CostEstimate(flops=10**9, bytes_accessed=2**22, transcendentals=0),
    )(own, other, cosine, sine)


def attend_kernel(count, groups, begin, *refs):
    firsts, refs = refs[:groups], refs[groups:]
    queries, refs = refs[:groups], refs[groups:]
    pieces, refs = refs[:count], refs[count:]
    if not begin:
        refs = refs[3 * groups :]
    states = [refs[3 * g : 3 * g + 3] for g in range(groups)]
    turned, bias, joined = refs[3 * groups :]
    if begin:
        for m_ref, l_ref, a_ref in states:
            m_ref[...] = jnp.full_like(m_ref, LOW)
            l_ref[...] = jnp.zeros_like(l_ref)
            a_ref[...] = jnp.zeros_like(a_ref)
    blocks = [p for p in pieces if p.shape[0] == BLOCK]
    filled = 0
    for piece in pieces:
        step = piece.shape[0]
        if step < BLOCK:
            joined[filled : filled + step, :] = piece[...]
            filled += step
            if filled % BLOCK == 0:
                blocks.append(joined.at[filled - BLOCK : filled])
    offsets = lax.broadcasted_iota(jnp.int32, (QROWS, BLOCK), 0)
    for keys in blocks:
        turned[...] = keys[...].T
        marks = turned[LAT + ROPE : LAT + ROPE + 16, :].astype(F32)
        key_pos = marks[0:1, :] * 128.0 + marks[1:2, :]
        for g in range(groups):
            query_pos = (firsts[g][0] + offsets).astype(F32)
            bias[g] = jnp.where(key_pos <= query_pos, 0.0, LOW)
        work = [(g, i) for g in range(groups) for i in range(ROWS // STEP)]

        def score(item):
            g, i = item
            s = jnp.dot(
                queries[g][i * STEP : (i + 1) * STEP, :],
                turned[...],
                preferred_element_type=F32,
            )
            s = s.reshape(STEP // QROWS, QROWS, BLOCK) + bias[g][None]
            return s.reshape(STEP, BLOCK)

        s = score(work[0])
        for n, (g, i) in enumerate(work):
            following = score(work[n + 1]) if n + 1 < len(work) else None
            m_ref, l_ref, a_ref = states[g]
            r = slice(i * STEP, (i + 1) * STEP)
            m_old = m_ref[r, :1]
            m_new = jnp.maximum(m_old, jnp.max(s, axis=1, keepdims=True))
            weights = jnp.exp2((s - m_new) * SCALE)
            fade = jnp.exp2((m_old - m_new) * SCALE)
            total = l_ref[r, :1] * fade + jnp.sum(weights, axis=1, keepdims=True)
            l_ref[r, :] = jnp.broadcast_to(total, (STEP, 128))
            m_ref[r, :] = jnp.broadcast_to(m_new, (STEP, 128))
            a_ref[r, :] = a_ref[r, :] * fade + jnp.dot(
                weights.astype(BF), keys[:, :LAT], preferred_element_type=F32
            )
            s = following


def attend(firsts, queries, pieces, states):
    groups = len(queries)
    begin = states is None
    total = sum(p.shape[0] for p in pieces)
    shapes = [
        pltpu.VMEM((ROWS, 128), F32),
        pltpu.VMEM((ROWS, 128), F32),
        pltpu.VMEM((ROWS, LAT), F32),
    ] * groups
    flat_states = [] if begin else [v for state in states for v in state]
    before = 2 * groups + len(pieces)
    out = pl.pallas_call(
        functools.partial(attend_kernel, len(pieces), groups, begin),
        out_shape=shapes,
        in_specs=[SMEM] * groups + [VMEM] * (groups + len(pieces) + len(flat_states)),
        out_specs=[VMEM] * (3 * groups),
        input_output_aliases={before + i: i for i in range(len(flat_states))},
        scratch_shapes=[
            pltpu.VMEM((WIDE, BLOCK), BF),
            pltpu.VMEM((groups, QROWS, BLOCK), F32),
            pltpu.VMEM((max(total, BLOCK), WIDE), BF),
        ],
        compiler_params=params(),
        cost_estimate=pl.CostEstimate(
            flops=2 * groups * ROWS * total * (WIDE + LAT) * 3 // (2 * 2),
            bytes_accessed=2 * total * WIDE // 2,
            transcendentals=0,
        ),
    )(*firsts, *queries, *pieces, *flat_states)
    return [tuple(out[3 * g : 3 * g + 3]) for g in range(groups)]


def pack_logs(logs):
    high = logs.astype(BF)
    left = logs - high.astype(F32)
    middle = left.astype(BF)
    low = (left - middle.astype(F32)).astype(BF)
    parts = [p.astype(F32)[:, :HEADS] for p in (high, middle, low)]
    rest = jnp.zeros((logs.shape[0], 128 - 3 * HEADS), F32)
    return jnp.concatenate(parts + [rest], axis=1).astype(BF)


def unpack_logs(packed):
    packed = packed.astype(F32)
    high, middle, low = (packed[:, i * HEADS : (i + 1) * HEADS] for i in range(3))
    return high + middle + low


WIDTH = HEADS * VD


def project_kernel(keep, m_ref, l_ref, a_ref, up_ref, other_up_ref, own_ref, other_ref, *stat):
    lane = lax.broadcasted_iota(jnp.int32, (QROWS, 128), 1)
    for side, (up, out) in enumerate(((up_ref, own_ref), (other_up_ref, other_ref))):
        logs = jnp.zeros((QROWS, 128), F32)
        for h in range(HEADS):
            rows = pl.ds((side * HEADS + h) * QROWS, QROWS)
            l = l_ref[rows, :1]
            latent = (a_ref[rows, :] / l).astype(BF)
            value = jnp.dot(latent, up[h], preferred_element_type=F32)
            out[:, h * VD : (h + 1) * VD] = value.astype(out.dtype)
            logs = jnp.where(lane == h, m_ref[rows, :1] * SCALE + jnp.log2(l), logs)
        if keep and not side:
            stat[0][...] = logs
        else:
            out[:, WIDTH:] = pack_logs(logs)


def project(keep, state, up, other_up):
    packed = jax.ShapeDtypeStruct((QROWS, WIDTH + 128), BF)
    shapes = [packed, packed]
    if keep:
        shapes = [
            jax.ShapeDtypeStruct((QROWS, WIDTH), F32),
            packed,
            jax.ShapeDtypeStruct((QROWS, 128), F32),
        ]
    return pl.pallas_call(
        functools.partial(project_kernel, keep),
        out_shape=shapes,
        in_specs=[VMEM] * 5,
        out_specs=[VMEM] * len(shapes),
        compiler_params=params(),
    )(*state, up, other_up)


def merge_kernel(own_ref, stat_ref, *refs):
    others, out_ref = refs[:-1], refs[-1]
    logs = [stat_ref[:, :HEADS]] + [unpack_logs(o[:, WIDTH:]) for o in others]
    top = functools.reduce(jnp.maximum, logs)
    shares = [jnp.exp2(v - top) for v in logs]
    total = functools.reduce(lambda a, b: a + b, shares)
    shares = [s / total for s in shares]
    for h in range(HEADS):
        c = slice(h * VD, (h + 1) * VD)
        value = own_ref[:, c] * shares[0][:, h : h + 1]
        for other, share in zip(others, shares[1:]):
            value = value + other[:, c].astype(F32) * share[:, h : h + 1]
        out_ref[:, c] = value.astype(BF)


def merge(own, stat, *others):
    return pl.pallas_call(
        merge_kernel,
        out_shape=jax.ShapeDtypeStruct((QROWS, WIDTH), BF),
        in_specs=[VMEM] * (2 + len(others)),
        out_specs=VMEM,
        compiler_params=params(),
    )(own, stat, *others)


def local(query_latent, query_rope, code_latent, code_rope, up_value, out_weight):
    z, xh, y, xl, core = (lax.axis_index(a) for a in AXES)
    row = z * 2 + xh
    pair_row = (z ^ 1) * 2 + xh
    col = (y * 2 + xl) * 2 + core
    key_first = (row * 16 + col) * QROWS
    query_first = 15360 + row * QROWS
    pair_first = 15360 + pair_row * QROWS
    key_first = key_first.reshape(1).astype(jnp.int32)
    first = query_first.reshape(1).astype(jnp.int32)
    second = pair_first.reshape(1).astype(jnp.int32)
    keys = make_keys(key_first, code_latent, code_rope, *table(key_first))
    column = jnp.concatenate([keys] + [move(keys, along_z(s)) for s in (4, 2, -2)], axis=0)

    queries = jnp.concatenate([query_latent, query_rope], axis=1)
    core_queries = move(queries, to_core)
    pair_queries = move(queries, to_pair)
    q1 = make_queries(queries, core_queries, *table(first))

    plane = jnp.concatenate([column] + [move(column, along_first(s)) for s in (2, 1, -1)], axis=0)
    plane, q1, pair_queries = lax.optimization_barrier((plane, q1, pair_queries))
    low, high = plane[: BLOCK // 2], plane[BLOCK // 2 :]
    early = [move(low, along_second(1)), move(high, along_second(-1))]
    far = [move(early[0], along_second(1)), move(early[1], along_second(-1))]
    both_queries = move(pair_queries, to_core)
    other_up = move(up_value, to_core)
    pair_weight = move(out_weight, to_pair)
    q2 = make_queries(pair_queries, both_queries, *table(second))

    (s1,) = attend([first], [q1], [plane], None)
    low, high, s1 = lax.optimization_barrier((low, high, s1))
    late = [move(high, along_second(1)), move(low, along_second(-1))]
    (s2,) = attend([second], [q2], [plane], None)
    s1, s2 = attend([first, second], [q1, q2], early, [s1, s2])
    (s2,) = attend([second], [q2], late, [s2])
    pair_weight, s2, *far = lax.optimization_barrier((pair_weight, s2, *far))
    side_weights = move(jnp.concatenate([out_weight, pair_weight], axis=0), along_x(2))
    (s2,) = attend([second], [q2], far, [s2])
    own2, other2 = project(False, s2, up_value, other_up)
    s1, own2, other2 = lax.optimization_barrier((s1, own2, other2))
    (s1,) = attend([first], [q1], [*late, *far], [s1])
    s1, *sent = lax.optimization_barrier((s1, move(own2, to_pair), move(other2, to_pair_core)))
    own1, other1, stat1 = project(True, s1, up_value, other_up)
    heads = merge(own1, stat1, move(other1, to_core), *sent)

    blocks = [heads, move(heads, along_z(2)), move(heads, along_z(4)), move(heads, along_z(-2))]
    same = xh == core
    sides = (side_weights[: HEADS * VD], side_weights[HEADS * VD :])
    keep_w = [jnp.where(same, o, s) for o, s in zip((out_weight, pair_weight), sides)]
    give_w = [jnp.where(same, s, o) for o, s in zip((out_weight, pair_weight), sides)]
    blocks[1], keep_w, give_w = lax.optimization_barrier((blocks[1], keep_w, give_w))
    found = jnp.concatenate(blocks, axis=0)
    give = jnp.stack([jnp.dot(found, w, preferred_element_type=F32).astype(BF) for w in give_w])
    keep = jnp.stack([jnp.dot(found, w, preferred_element_type=F32) for w in keep_w])
    columns = out_weight.shape[1]
    part = (keep + move(give, to_core).astype(F32)).reshape(2, 4, QROWS, columns)
    sent = part.astype(BF)
    total = None
    for dy in (2, 1, 3, 0):
        block = (z // 2 - (y + dy)) % 4
        if dy:
            got = move(lax.dynamic_index_in_dim(sent, block, 1, False), along_y(dy)).astype(F32)
        else:
            got = lax.dynamic_index_in_dim(part, block, 1, False)
        total = got if total is None else total + got
    total = total.astype(BF)
    result = None
    for s in (0, 1):

        def target(z, x, y, core):
            return (z & 6) | ((x & 1) ^ s), core * 2 + (z & 1), y, x >> 1

        piece = lax.dynamic_index_in_dim(total, (xl ^ s) ^ (z & 1), 0, False)
        got = move(piece, target).astype(F32)
        result = got if result is None else result + got
    return result.astype(BF)


def solution(mesh):
    fine = Mesh(mesh.devices.reshape(8, 2, 4, 2, 2), AXES)
    row, col = ("z", "xh"), ("y", "xl", "core")
    in_specs = (P(row, col), P(row, col), P(row + col, None), P(row + col, None), P(col, None, None), P(col, row))
    return jax.shard_map(local, mesh=fine, in_specs=in_specs, out_specs=P(col, row), check_vma=False)
```

```python
import functools
import math

import jax
import jax.numpy as jnp
from jax import lax
from jax.experimental import pallas as pl
from jax.experimental.pallas import tpu as pltpu
from jax.sharding import Mesh, PartitionSpec as P

ROPE = 64
NOPE = 128
LAT = 512
VD = 128
HEADS = 8
QROWS = 64
WIDE = 640
SCALE = math.log2(math.e) / math.sqrt(NOPE + ROPE)
LOW = -1e30
VMEM = pl.BlockSpec(memory_space=pltpu.VMEM)
SMEM = pl.BlockSpec(memory_space=pltpu.SMEM)
ROWS = 2 * HEADS * QROWS
STEP = 256
BLOCK = 1024
BF = jnp.bfloat16
F32 = jnp.float32
AXES = ("z", "xh", "y", "xl", "core")


def flat(z, x, y, core):
    return (((z * 2 + x // 2) * 4 + y) * 2 + x % 2) * 2 + core


def move(value, target):
    perm = []
    for z in range(8):
        for x in range(4):
            for y in range(4):
                for core in range(2):
                    perm.append((flat(z, x, y, core), flat(*target(z, x, y, core))))
    return lax.ppermute(value, AXES, perm)


def to_core(z, x, y, core):
    return z, x, y, 1 - core


def to_pair(z, x, y, core):
    return z ^ 1, x, y, core


def to_pair_core(z, x, y, core):
    return z ^ 1, x, y, 1 - core


def along_z(step):
    return lambda z, x, y, core: ((z + step) % 8, x, y, core)


def along_y(step):
    return lambda z, x, y, core: (z, x, (y + step) % 4, core)


def along_x(step):
    return lambda z, x, y, core: (z, (x + step) % 4, y, core)


def along_first(step):
    return lambda z, x, y, core: (
        (z, (x + step) % 4, y, core) if core else (z, x, (y + step) % 4, core)
    )


def along_second(step):
    return lambda z, x, y, core: (
        (z, x, (y + step) % 4, core) if core else (z, (x + step) % 4, y, core)
    )


def params(mib=32):
    return pltpu.CompilerParams(vmem_limit_bytes=mib * 2**20)


def table(first):
    lane = jnp.arange(128, dtype=jnp.int32)
    half = ROPE // 2
    inverse = 10000.0 ** (-(lane % half).astype(F32) / half)
    angles = (first + jnp.arange(QROWS, dtype=jnp.int32)).astype(F32)[:, None] * inverse[None, :]
    sign = jnp.where(lane % ROPE < half, -1.0, 1.0)
    return jnp.cos(angles), jnp.sin(angles) * sign[None, :]


def key_kernel(first_ref, latent_ref, rope_ref, cos_ref, sin_ref, out_ref):
    half = ROPE // 2
    out_ref[:, :LAT] = latent_ref[...]
    values = rope_ref[...].astype(F32)
    a, b = values[:, :half], values[:, half:]
    cosine, sine = cos_ref[:, :half], sin_ref[:, half:ROPE]
    lane = lax.broadcasted_iota(jnp.int32, (QROWS, ROPE), 1)
    pos = first_ref[0] + lax.broadcasted_iota(jnp.int32, (QROWS, ROPE), 0)
    marks = jnp.where(lane == 0, pos // 128, jnp.where(lane == 1, pos % 128, 0)).astype(F32)
    out_ref[:, LAT:] = jnp.concatenate(
        [a * cosine - b * sine, b * cosine + a * sine, marks], axis=1
    ).astype(BF)


def make_keys(first, latent, rope, cosine, sine):
    return pl.pallas_call(
        key_kernel,
        out_shape=jax.ShapeDtypeStruct((QROWS, WIDE), BF),
        in_specs=[SMEM] + [VMEM] * 4,
        out_specs=VMEM,
        compiler_params=params(),
    )(first, latent, rope, cosine, sine)


def query_kernel(own_ref, other_ref, cos_ref, sin_ref, out_ref):
    lane = lax.broadcasted_iota(jnp.int32, (QROWS, 128), 1)
    for side, ref in enumerate((own_ref, other_ref)):
        for h in range(0, HEADS, 2):
            start = HEADS * LAT + h * ROPE
            pair = ref[:, start : start + 2 * ROPE].astype(F32)
            swapped = jnp.where(
                lane % ROPE < ROPE // 2, pltpu.roll(pair, 96, 1), pltpu.roll(pair, 32, 1)
            )
            turned = pair * cos_ref[...] + swapped * sin_ref[...]
            for k, value in enumerate((turned, pltpu.roll(turned, ROPE, 1))):
                rows = pl.ds((side * HEADS + h + k) * QROWS, QROWS)
                out_ref[rows, :LAT] = ref[:, (h + k) * LAT : (h + k + 1) * LAT]
                out_ref[rows, LAT:] = jnp.where(lane < ROPE, value, 0.0).astype(BF)


def make_queries(own, other, cosine, sine):
    return pl.pallas_call(
        query_kernel,
        out_shape=pltpu.VMEM((ROWS, WIDE), BF),
        in_specs=[VMEM] * 4,
        out_specs=VMEM,
        compiler_params=params(),
        cost_estimate=pl.CostEstimate(flops=10**9, bytes_accessed=2**22, transcendentals=0),
    )(own, other, cosine, sine)


def attend_kernel(count, groups, begin, *refs):
    firsts, refs = refs[:groups], refs[groups:]
    queries, refs = refs[:groups], refs[groups:]
    pieces, refs = refs[:count], refs[count:]
    if not begin:
        refs = refs[3 * groups :]
    states = [refs[3 * g : 3 * g + 3] for g in range(groups)]
    turned, bias, joined = refs[3 * groups :]
    if begin:
        for m_ref, l_ref, a_ref in states:
            m_ref[...] = jnp.full_like(m_ref, LOW)
            l_ref[...] = jnp.zeros_like(l_ref)
            a_ref[...] = jnp.zeros_like(a_ref)
    blocks = [p for p in pieces if p.shape[0] == BLOCK]
    filled = 0
    for piece in pieces:
        step = piece.shape[0]
        if step < BLOCK:
            joined[filled : filled + step, :] = piece[...]
            filled += step
            if filled % BLOCK == 0:
                blocks.append(joined.at[filled - BLOCK : filled])
    offsets = lax.broadcasted_iota(jnp.int32, (QROWS, BLOCK), 0)
    for keys in blocks:
        turned[...] = keys[...].T
        marks = turned[LAT + ROPE : LAT + ROPE + 16, :].astype(F32)
        key_pos = marks[0:1, :] * 128.0 + marks[1:2, :]
        for g in range(groups):
            query_pos = (firsts[g][0] + offsets).astype(F32)
            bias[g] = jnp.where(key_pos <= query_pos, 0.0, LOW)
        work = [(g, i) for g in range(groups) for i in range(ROWS // STEP)]

        def score(item):
            g, i = item
            s = jnp.dot(
                queries[g][i * STEP : (i + 1) * STEP, :],
                turned[...],
                preferred_element_type=F32,
            )
            s = s.reshape(STEP // QROWS, QROWS, BLOCK) + bias[g][None]
            return s.reshape(STEP, BLOCK)

        s = score(work[0])
        for n, (g, i) in enumerate(work):
            following = score(work[n + 1]) if n + 1 < len(work) else None
            m_ref, l_ref, a_ref = states[g]
            r = slice(i * STEP, (i + 1) * STEP)
            m_old = m_ref[r, :1]
            m_new = jnp.maximum(m_old, jnp.max(s, axis=1, keepdims=True))
            weights = jnp.exp2((s - m_new) * SCALE)
            fade = jnp.exp2((m_old - m_new) * SCALE)
            total = l_ref[r, :1] * fade + jnp.sum(weights, axis=1, keepdims=True)
            l_ref[r, :] = jnp.broadcast_to(total, (STEP, 128))
            m_ref[r, :] = jnp.broadcast_to(m_new, (STEP, 128))
            a_ref[r, :] = a_ref[r, :] * fade + jnp.dot(
                weights.astype(BF), keys[:, :LAT], preferred_element_type=F32
            )
            s = following


def attend(firsts, queries, pieces, states):
    groups = len(queries)
    begin = states is None
    total = sum(p.shape[0] for p in pieces)
    shapes = [
        pltpu.VMEM((ROWS, 128), F32),
        pltpu.VMEM((ROWS, 128), F32),
        pltpu.VMEM((ROWS, LAT), F32),
    ] * groups
    flat_states = [] if begin else [v for state in states for v in state]
    before = 2 * groups + len(pieces)
    out = pl.pallas_call(
        functools.partial(attend_kernel, len(pieces), groups, begin),
        out_shape=shapes,
        in_specs=[SMEM] * groups + [VMEM] * (groups + len(pieces) + len(flat_states)),
        out_specs=[VMEM] * (3 * groups),
        input_output_aliases={before + i: i for i in range(len(flat_states))},
        scratch_shapes=[
            pltpu.VMEM((WIDE, BLOCK), BF),
            pltpu.VMEM((groups, QROWS, BLOCK), F32),
            pltpu.VMEM((max(total, BLOCK), WIDE), BF),
        ],
        compiler_params=params(),
        cost_estimate=pl.CostEstimate(
            flops=2 * groups * ROWS * total * (WIDE + LAT) * 3 // (2 * 2),
            bytes_accessed=2 * total * WIDE // 2,
            transcendentals=0,
        ),
    )(*firsts, *queries, *pieces, *flat_states)
    return [tuple(out[3 * g : 3 * g + 3]) for g in range(groups)]


def pack_logs(logs):
    high = logs.astype(BF)
    left = logs - high.astype(F32)
    middle = left.astype(BF)
    low = (left - middle.astype(F32)).astype(BF)
    parts = [p.astype(F32)[:, :HEADS] for p in (high, middle, low)]
    rest = jnp.zeros((logs.shape[0], 128 - 3 * HEADS), F32)
    return jnp.concatenate(parts + [rest], axis=1).astype(BF)


def unpack_logs(packed):
    packed = packed.astype(F32)
    high, middle, low = (packed[:, i * HEADS : (i + 1) * HEADS] for i in range(3))
    return high + middle + low


WIDTH = HEADS * VD


def project_kernel(keep, m_ref, l_ref, a_ref, up_ref, other_up_ref, own_ref, other_ref, *stat):
    lane = lax.broadcasted_iota(jnp.int32, (QROWS, 128), 1)
    for side, (up, out) in enumerate(((up_ref, own_ref), (other_up_ref, other_ref))):
        logs = jnp.zeros((QROWS, 128), F32)
        for h in range(HEADS):
            rows = pl.ds((side * HEADS + h) * QROWS, QROWS)
            l = l_ref[rows, :1]
            latent = (a_ref[rows, :] / l).astype(BF)
            value = jnp.dot(latent, up[h], preferred_element_type=F32)
            out[:, h * VD : (h + 1) * VD] = value.astype(out.dtype)
            logs = jnp.where(lane == h, m_ref[rows, :1] * SCALE + jnp.log2(l), logs)
        if keep and not side:
            stat[0][...] = logs
        else:
            out[:, WIDTH:] = pack_logs(logs)


def project(keep, state, up, other_up):
    packed = jax.ShapeDtypeStruct((QROWS, WIDTH + 128), BF)
    shapes = [packed, packed]
    if keep:
        shapes = [
            jax.ShapeDtypeStruct((QROWS, WIDTH), F32),
            packed,
            jax.ShapeDtypeStruct((QROWS, 128), F32),
        ]
    return pl.pallas_call(
        functools.partial(project_kernel, keep),
        out_shape=shapes,
        in_specs=[VMEM] * 5,
        out_specs=[VMEM] * len(shapes),
        compiler_params=params(),
    )(*state, up, other_up)


def merge_kernel(own_ref, stat_ref, *refs):
    others, out_ref = refs[:-1], refs[-1]
    logs = [stat_ref[:, :HEADS]] + [unpack_logs(o[:, WIDTH:]) for o in others]
    top = functools.reduce(jnp.maximum, logs)
    shares = [jnp.exp2(v - top) for v in logs]
    total = functools.reduce(lambda a, b: a + b, shares)
    shares = [s / total for s in shares]
    for h in range(HEADS):
        c = slice(h * VD, (h + 1) * VD)
        value = own_ref[:, c] * shares[0][:, h : h + 1]
        for other, share in zip(others, shares[1:]):
            value = value + other[:, c].astype(F32) * share[:, h : h + 1]
        out_ref[:, c] = value.astype(BF)


def merge(own, stat, *others):
    return pl.pallas_call(
        merge_kernel,
        out_shape=jax.ShapeDtypeStruct((QROWS, WIDTH), BF),
        in_specs=[VMEM] * (2 + len(others)),
        out_specs=VMEM,
        compiler_params=params(),
    )(own, stat, *others)


def local(query_latent, query_rope, code_latent, code_rope, up_value, out_weight):
    z, xh, y, xl, core = (lax.axis_index(a) for a in AXES)
    row = z * 2 + xh
    pair_row = (z ^ 1) * 2 + xh
    col = (y * 2 + xl) * 2 + core
    key_first = (row * 16 + col) * QROWS
    query_first = 15360 + row * QROWS
    pair_first = 15360 + pair_row * QROWS
    key_first = key_first.reshape(1).astype(jnp.int32)
    first = query_first.reshape(1).astype(jnp.int32)
    second = pair_first.reshape(1).astype(jnp.int32)
    keys = make_keys(key_first, code_latent, code_rope, *table(key_first))
    column = jnp.concatenate([keys] + [move(keys, along_z(s)) for s in (4, 2, -2)], axis=0)

    queries = jnp.concatenate([query_latent, query_rope], axis=1)
    core_queries = move(queries, to_core)
    pair_queries = move(queries, to_pair)
    q1 = make_queries(queries, core_queries, *table(first))

    plane = jnp.concatenate([column] + [move(column, along_first(s)) for s in (2, 1, -1)], axis=0)
    plane, q1, pair_queries = lax.optimization_barrier((plane, q1, pair_queries))
    low, high = plane[: BLOCK // 2], plane[BLOCK // 2 :]
    early = [move(low, along_second(1)), move(high, along_second(-1))]
    both_queries = move(pair_queries, to_core)
    other_up = move(up_value, to_core)
    pair_weight = move(out_weight, to_pair)
    q2 = make_queries(pair_queries, both_queries, *table(second))

    (s1,) = attend([first], [q1], [plane], None)
    low, high, s1 = lax.optimization_barrier((low, high, s1))
    late = [move(high, along_second(1)), move(low, along_second(-1))]
    (s2,) = attend([second], [q2], [plane], None)
    s2, *early = lax.optimization_barrier((s2, *early))
    far = [move(early[0], along_second(1)), move(early[1], along_second(-1))]
    s1, s2 = attend([first, second], [q1, q2], early, [s1, s2])
    (s2,) = attend([second], [q2], late, [s2])
    pair_weight, s2, *far = lax.optimization_barrier((pair_weight, s2, *far))
    side_weights = move(jnp.concatenate([out_weight, pair_weight], axis=0), along_x(2))
    (s2,) = attend([second], [q2], far, [s2])
    own2, other2 = project(False, s2, up_value, other_up)
    s1, own2, other2 = lax.optimization_barrier((s1, own2, other2))
    (s1,) = attend([first], [q1], [*late, *far], [s1])
    s1, *sent = lax.optimization_barrier((s1, move(own2, to_pair), move(other2, to_pair_core)))
    own1, other1, stat1 = project(True, s1, up_value, other_up)
    heads = merge(own1, stat1, move(other1, to_core), *sent)

    blocks = [heads, move(heads, along_z(2)), move(heads, along_z(4)), move(heads, along_z(-2))]
    same = xh == core
    sides = (side_weights[: HEADS * VD], side_weights[HEADS * VD :])
    keep_w = [jnp.where(same, o, s) for o, s in zip((out_weight, pair_weight), sides)]
    give_w = [jnp.where(same, s, o) for o, s in zip((out_weight, pair_weight), sides)]
    blocks[2], keep_w, give_w = lax.optimization_barrier((blocks[2], keep_w, give_w))
    found = jnp.concatenate(blocks, axis=0)
    give = jnp.stack([jnp.dot(found, w, preferred_element_type=F32).astype(BF) for w in give_w])
    keep = jnp.stack([jnp.dot(found, w, preferred_element_type=F32) for w in keep_w])
    columns = out_weight.shape[1]
    part = (keep + move(give, to_core).astype(F32)).reshape(2, 4, QROWS, columns)
    sent = part.astype(BF)
    total = None
    for dy in (2, 1, 3, 0):
        block = (z // 2 - (y + dy)) % 4
        if dy:
            got = move(lax.dynamic_index_in_dim(sent, block, 1, False), along_y(dy)).astype(F32)
        else:
            got = lax.dynamic_index_in_dim(part, block, 1, False)
        total = got if total is None else total + got
    total = total.astype(BF)
    result = None
    for s in (0, 1):

        def target(z, x, y, core):
            return (z & 6) | ((x & 1) ^ s), core * 2 + (z & 1), y, x >> 1

        piece = lax.dynamic_index_in_dim(total, (xl ^ s) ^ (z & 1), 0, False)
        got = move(piece, target).astype(F32)
        result = got if result is None else result + got
    return result.astype(BF)


def solution(mesh):
    fine = Mesh(mesh.devices.reshape(8, 2, 4, 2, 2), AXES)
    row, col = ("z", "xh"), ("y", "xl", "core")
    in_specs = (P(row, col), P(row, col), P(row + col, None), P(row + col, None), P(col, None, None), P(col, row))
    return jax.shard_map(local, mesh=fine, in_specs=in_specs, out_specs=P(col, row), check_vma=False)
```

```python
import functools
import math

import jax
import jax.numpy as jnp
from jax import lax
from jax.experimental import pallas as pl
from jax.experimental.pallas import tpu as pltpu
from jax.sharding import Mesh, PartitionSpec as P

ROPE = 64
NOPE = 128
LAT = 512
VD = 128
HEADS = 8
QROWS = 64
WIDE = 640
SCALE = math.log2(math.e) / math.sqrt(NOPE + ROPE)
LOW = -1e30
VMEM = pl.BlockSpec(memory_space=pltpu.VMEM)
SMEM = pl.BlockSpec(memory_space=pltpu.SMEM)
HBM = pl.BlockSpec(memory_space=pltpu.HBM)
ROWS = 2 * HEADS * QROWS
STEP = 256
BLOCK = 1024
BF = jnp.bfloat16
F32 = jnp.float32
AXES = ("z", "xh", "y", "xl", "core")


def flat(z, x, y, core):
    return (((z * 2 + x // 2) * 4 + y) * 2 + x % 2) * 2 + core


def move(value, target):
    perm = []
    for z in range(8):
        for x in range(4):
            for y in range(4):
                for core in range(2):
                    perm.append((flat(z, x, y, core), flat(*target(z, x, y, core))))
    return lax.ppermute(value, AXES, perm)


def to_core(z, x, y, core):
    return z, x, y, 1 - core


def to_pair(z, x, y, core):
    return z ^ 1, x, y, core


def to_pair_core(z, x, y, core):
    return z ^ 1, x, y, 1 - core


def along_z(step):
    return lambda z, x, y, core: ((z + step) % 8, x, y, core)


def along_y(step):
    return lambda z, x, y, core: (z, x, (y + step) % 4, core)


def along_x(step):
    return lambda z, x, y, core: (z, (x + step) % 4, y, core)


def along_first(step):
    return lambda z, x, y, core: (
        (z, (x + step) % 4, y, core) if core else (z, x, (y + step) % 4, core)
    )


def along_second(step):
    return lambda z, x, y, core: (
        (z, x, (y + step) % 4, core) if core else (z, (x + step) % 4, y, core)
    )


def params(mib=32):
    return pltpu.CompilerParams(vmem_limit_bytes=mib * 2**20)


def table(first):
    lane = jnp.arange(128, dtype=jnp.int32)
    half = ROPE // 2
    inverse = 10000.0 ** (-(lane % half).astype(F32) / half)
    angles = (first + jnp.arange(QROWS, dtype=jnp.int32)).astype(F32)[:, None] * inverse[None, :]
    sign = jnp.where(lane % ROPE < half, -1.0, 1.0)
    return jnp.cos(angles), jnp.sin(angles) * sign[None, :]


def key_kernel(first_ref, latent_hbm, rope_hbm, cos_ref, sin_ref, out_ref, latent_ref, rope_ref, sems):
    half = ROPE // 2
    latent_copy = pltpu.make_async_copy(latent_hbm, latent_ref, sems.at[0])
    rope_copy = pltpu.make_async_copy(rope_hbm, rope_ref, sems.at[1])
    latent_copy.start()
    rope_copy.start()
    rope_copy.wait()
    latent_copy.wait()
    out_ref[:, :LAT] = latent_ref[...]
    values = rope_ref[...].astype(F32)
    a, b = values[:, :half], values[:, half:]
    cosine, sine = cos_ref[:, :half], sin_ref[:, half:ROPE]
    lane = lax.broadcasted_iota(jnp.int32, (QROWS, ROPE), 1)
    pos = first_ref[0] + lax.broadcasted_iota(jnp.int32, (QROWS, ROPE), 0)
    marks = jnp.where(lane == 0, pos // 128, jnp.where(lane == 1, pos % 128, 0)).astype(F32)
    out_ref[:, LAT:] = jnp.concatenate(
        [a * cosine - b * sine, b * cosine + a * sine, marks], axis=1
    ).astype(BF)


def make_keys(first, latent, rope, cosine, sine):
    return pl.pallas_call(
        key_kernel,
        out_shape=jax.ShapeDtypeStruct((QROWS, WIDE), BF),
        in_specs=[SMEM, HBM, HBM, VMEM, VMEM],
        out_specs=VMEM,
        scratch_shapes=[
            pltpu.VMEM((QROWS, LAT), BF),
            pltpu.VMEM((QROWS, ROPE), BF),
            pltpu.SemaphoreType.DMA((2,)),
        ],
        compiler_params=params(),
    )(first, latent, rope, cosine, sine)


def query_kernel(own_ref, other_ref, cos_ref, sin_ref, out_ref):
    lane = lax.broadcasted_iota(jnp.int32, (QROWS, 128), 1)
    for side, ref in enumerate((own_ref, other_ref)):
        for h in range(0, HEADS, 2):
            start = HEADS * LAT + h * ROPE
            pair = ref[:, start : start + 2 * ROPE].astype(F32)
            swapped = jnp.where(
                lane % ROPE < ROPE // 2, pltpu.roll(pair, 96, 1), pltpu.roll(pair, 32, 1)
            )
            turned = pair * cos_ref[...] + swapped * sin_ref[...]
            for k, value in enumerate((turned, pltpu.roll(turned, ROPE, 1))):
                rows = pl.ds((side * HEADS + h + k) * QROWS, QROWS)
                out_ref[rows, :LAT] = ref[:, (h + k) * LAT : (h + k + 1) * LAT]
                out_ref[rows, LAT:] = jnp.where(lane < ROPE, value, 0.0).astype(BF)


def make_queries(own, other, cosine, sine):
    return pl.pallas_call(
        query_kernel,
        out_shape=pltpu.VMEM((ROWS, WIDE), BF),
        in_specs=[VMEM] * 4,
        out_specs=VMEM,
        compiler_params=params(),
        cost_estimate=pl.CostEstimate(flops=10**9, bytes_accessed=2**22, transcendentals=0),
    )(own, other, cosine, sine)


def attend_kernel(count, groups, begin, *refs):
    firsts, refs = refs[:groups], refs[groups:]
    queries, refs = refs[:groups], refs[groups:]
    pieces, refs = refs[:count], refs[count:]
    if not begin:
        refs = refs[3 * groups :]
    states = [refs[3 * g : 3 * g + 3] for g in range(groups)]
    turned, bias, joined = refs[3 * groups :]
    if begin:
        for m_ref, l_ref, a_ref in states:
            m_ref[...] = jnp.full_like(m_ref, LOW)
            l_ref[...] = jnp.zeros_like(l_ref)
            a_ref[...] = jnp.zeros_like(a_ref)
    blocks = [p for p in pieces if p.shape[0] == BLOCK]
    filled = 0
    for piece in pieces:
        step = piece.shape[0]
        if step < BLOCK:
            joined[filled : filled + step, :] = piece[...]
            filled += step
            if filled % BLOCK == 0:
                blocks.append(joined.at[filled - BLOCK : filled])
    offsets = lax.broadcasted_iota(jnp.int32, (QROWS, BLOCK), 0)
    for keys in blocks:
        turned[...] = keys[...].T
        marks = turned[LAT + ROPE : LAT + ROPE + 16, :].astype(F32)
        key_pos = marks[0:1, :] * 128.0 + marks[1:2, :]
        for g in range(groups):
            query_pos = (firsts[g][0] + offsets).astype(F32)
            bias[g] = jnp.where(key_pos <= query_pos, 0.0, LOW)
        work = [(g, i) for g in range(groups) for i in range(ROWS // STEP)]

        def score(item):
            g, i = item
            s = jnp.dot(
                queries[g][i * STEP : (i + 1) * STEP, :],
                turned[...],
                preferred_element_type=F32,
            )
            s = s.reshape(STEP // QROWS, QROWS, BLOCK) + bias[g][None]
            return s.reshape(STEP, BLOCK)

        s = score(work[0])
        for n, (g, i) in enumerate(work):
            following = score(work[n + 1]) if n + 1 < len(work) else None
            m_ref, l_ref, a_ref = states[g]
            r = slice(i * STEP, (i + 1) * STEP)
            m_old = m_ref[r, :1]
            m_new = jnp.maximum(m_old, jnp.max(s, axis=1, keepdims=True))
            weights = jnp.exp2((s - m_new) * SCALE)
            fade = jnp.exp2((m_old - m_new) * SCALE)
            total = l_ref[r, :1] * fade + jnp.sum(weights, axis=1, keepdims=True)
            l_ref[r, :] = jnp.broadcast_to(total, (STEP, 128))
            m_ref[r, :] = jnp.broadcast_to(m_new, (STEP, 128))
            a_ref[r, :] = a_ref[r, :] * fade + jnp.dot(
                weights.astype(BF), keys[:, :LAT], preferred_element_type=F32
            )
            s = following


def attend(firsts, queries, pieces, states):
    groups = len(queries)
    begin = states is None
    total = sum(p.shape[0] for p in pieces)
    shapes = [
        pltpu.VMEM((ROWS, 128), F32),
        pltpu.VMEM((ROWS, 128), F32),
        pltpu.VMEM((ROWS, LAT), F32),
    ] * groups
    flat_states = [] if begin else [v for state in states for v in state]
    before = 2 * groups + len(pieces)
    out = pl.pallas_call(
        functools.partial(attend_kernel, len(pieces), groups, begin),
        out_shape=shapes,
        in_specs=[SMEM] * groups + [VMEM] * (groups + len(pieces) + len(flat_states)),
        out_specs=[VMEM] * (3 * groups),
        input_output_aliases={before + i: i for i in range(len(flat_states))},
        scratch_shapes=[
            pltpu.VMEM((WIDE, BLOCK), BF),
            pltpu.VMEM((groups, QROWS, BLOCK), F32),
            pltpu.VMEM((max(total, BLOCK), WIDE), BF),
        ],
        compiler_params=params(),
        cost_estimate=pl.CostEstimate(
            flops=2 * groups * ROWS * total * (WIDE + LAT) * 3 // (2 * 2),
            bytes_accessed=2 * total * WIDE // 2,
            transcendentals=0,
        ),
    )(*firsts, *queries, *pieces, *flat_states)
    return [tuple(out[3 * g : 3 * g + 3]) for g in range(groups)]


def pack_logs(logs):
    high = logs.astype(BF)
    left = logs - high.astype(F32)
    middle = left.astype(BF)
    low = (left - middle.astype(F32)).astype(BF)
    parts = [p.astype(F32)[:, :HEADS] for p in (high, middle, low)]
    rest = jnp.zeros((logs.shape[0], 128 - 3 * HEADS), F32)
    return jnp.concatenate(parts + [rest], axis=1).astype(BF)


def unpack_logs(packed):
    packed = packed.astype(F32)
    high, middle, low = (packed[:, i * HEADS : (i + 1) * HEADS] for i in range(3))
    return high + middle + low


WIDTH = HEADS * VD


def project_kernel(keep, m_ref, l_ref, a_ref, up_ref, other_up_ref, own_ref, other_ref, *stat):
    lane = lax.broadcasted_iota(jnp.int32, (QROWS, 128), 1)
    for side, (up, out) in enumerate(((up_ref, own_ref), (other_up_ref, other_ref))):
        logs = jnp.zeros((QROWS, 128), F32)
        for h in range(HEADS):
            rows = pl.ds((side * HEADS + h) * QROWS, QROWS)
            l = l_ref[rows, :1]
            latent = (a_ref[rows, :] / l).astype(BF)
            value = jnp.dot(latent, up[h], preferred_element_type=F32)
            out[:, h * VD : (h + 1) * VD] = value.astype(out.dtype)
            logs = jnp.where(lane == h, m_ref[rows, :1] * SCALE + jnp.log2(l), logs)
        if keep and not side:
            stat[0][...] = logs
        else:
            out[:, WIDTH:] = pack_logs(logs)


def project(keep, state, up, other_up):
    packed = jax.ShapeDtypeStruct((QROWS, WIDTH + 128), BF)
    shapes = [packed, packed]
    if keep:
        shapes = [
            jax.ShapeDtypeStruct((QROWS, WIDTH), F32),
            packed,
            jax.ShapeDtypeStruct((QROWS, 128), F32),
        ]
    return pl.pallas_call(
        functools.partial(project_kernel, keep),
        out_shape=shapes,
        in_specs=[VMEM] * 5,
        out_specs=[VMEM] * len(shapes),
        compiler_params=params(),
    )(*state, up, other_up)


def merge_kernel(own_ref, stat_ref, *refs):
    others, out_ref = refs[:-1], refs[-1]
    logs = [stat_ref[:, :HEADS]] + [unpack_logs(o[:, WIDTH:]) for o in others]
    top = functools.reduce(jnp.maximum, logs)
    shares = [jnp.exp2(v - top) for v in logs]
    total = functools.reduce(lambda a, b: a + b, shares)
    shares = [s / total for s in shares]
    for h in range(HEADS):
        c = slice(h * VD, (h + 1) * VD)
        value = own_ref[:, c] * shares[0][:, h : h + 1]
        for other, share in zip(others, shares[1:]):
            value = value + other[:, c].astype(F32) * share[:, h : h + 1]
        out_ref[:, c] = value.astype(BF)


def merge(own, stat, *others):
    return pl.pallas_call(
        merge_kernel,
        out_shape=jax.ShapeDtypeStruct((QROWS, WIDTH), BF),
        in_specs=[VMEM] * (2 + len(others)),
        out_specs=VMEM,
        compiler_params=params(),
    )(own, stat, *others)


def local(query_latent, query_rope, code_latent, code_rope, up_value, out_weight):
    z, xh, y, xl, core = (lax.axis_index(a) for a in AXES)
    row = z * 2 + xh
    pair_row = (z ^ 1) * 2 + xh
    col = (y * 2 + xl) * 2 + core
    key_first = (row * 16 + col) * QROWS
    query_first = 15360 + row * QROWS
    pair_first = 15360 + pair_row * QROWS
    key_first = key_first.reshape(1).astype(jnp.int32)
    first = query_first.reshape(1).astype(jnp.int32)
    second = pair_first.reshape(1).astype(jnp.int32)
    keys = make_keys(key_first, code_latent, code_rope, *table(key_first))
    column = jnp.concatenate([keys] + [move(keys, along_z(s)) for s in (4, 2, -2)], axis=0)

    queries = jnp.concatenate([query_latent, query_rope], axis=1)
    core_queries = move(queries, to_core)
    pair_queries = move(queries, to_pair)
    q1 = make_queries(queries, core_queries, *table(first))

    plane = jnp.concatenate([column] + [move(column, along_first(s)) for s in (2, 1, -1)], axis=0)
    plane, q1, pair_queries = lax.optimization_barrier((plane, q1, pair_queries))
    low, high = plane[: BLOCK // 2], plane[BLOCK // 2 :]
    early = [move(low, along_second(1)), move(high, along_second(-1))]
    both_queries = move(pair_queries, to_core)
    other_up = move(up_value, to_core)
    pair_weight = move(out_weight, to_pair)
    q2 = make_queries(pair_queries, both_queries, *table(second))

    (s1,) = attend([first], [q1], [plane], None)
    low, high, s1 = lax.optimization_barrier((low, high, s1))
    late = [move(high, along_second(1)), move(low, along_second(-1))]
    (s2,) = attend([second], [q2], [plane], None)
    s2, *early = lax.optimization_barrier((s2, *early))
    far = [move(early[0], along_second(1)), move(early[1], along_second(-1))]
    s1, s2 = attend([first, second], [q1, q2], early, [s1, s2])
    (s2,) = attend([second], [q2], late, [s2])
    pair_weight, s2, *far = lax.optimization_barrier((pair_weight, s2, *far))
    side_weights = move(jnp.concatenate([out_weight, pair_weight], axis=0), along_x(2))
    (s2,) = attend([second], [q2], far, [s2])
    own2, other2 = project(False, s2, up_value, other_up)
    s1, own2, other2 = lax.optimization_barrier((s1, own2, other2))
    (s1,) = attend([first], [q1], [*late, *far], [s1])
    s1, *sent = lax.optimization_barrier((s1, move(own2, to_pair), move(other2, to_pair_core)))
    own1, other1, stat1 = project(True, s1, up_value, other_up)
    heads = merge(own1, stat1, move(other1, to_core), *sent)

    blocks = [heads, move(heads, along_z(2)), move(heads, along_z(4)), move(heads, along_z(-2))]
    same = xh == core
    sides = (side_weights[: HEADS * VD], side_weights[HEADS * VD :])
    keep_w = [jnp.where(same, o, s) for o, s in zip((out_weight, pair_weight), sides)]
    give_w = [jnp.where(same, s, o) for o, s in zip((out_weight, pair_weight), sides)]
    blocks[2], keep_w, give_w = lax.optimization_barrier((blocks[2], keep_w, give_w))
    found = jnp.concatenate(blocks, axis=0)
    give = jnp.stack([jnp.dot(found, w, preferred_element_type=F32).astype(BF) for w in give_w])
    keep = jnp.stack([jnp.dot(found, w, preferred_element_type=F32) for w in keep_w])
    columns = out_weight.shape[1]
    part = (keep + move(give, to_core).astype(F32)).reshape(2, 4, QROWS, columns)
    sent = part.astype(BF)
    total = None
    for dy in (2, 1, 3, 0):
        block = (z // 2 - (y + dy)) % 4
        if dy:
            got = move(lax.dynamic_index_in_dim(sent, block, 1, False), along_y(dy)).astype(F32)
        else:
            got = lax.dynamic_index_in_dim(part, block, 1, False)
        total = got if total is None else total + got
    total = total.astype(BF)
    result = None
    for s in (0, 1):

        def target(z, x, y, core):
            return (z & 6) | ((x & 1) ^ s), core * 2 + (z & 1), y, x >> 1

        piece = lax.dynamic_index_in_dim(total, (xl ^ s) ^ (z & 1), 0, False)
        got = move(piece, target).astype(F32)
        result = got if result is None else result + got
    return result.astype(BF)


def solution(mesh):
    fine = Mesh(mesh.devices.reshape(8, 2, 4, 2, 2), AXES)
    row, col = ("z", "xh"), ("y", "xl", "core")
    in_specs = (P(row, col), P(row, col), P(row + col, None), P(row + col, None), P(col, None, None), P(col, row))
    return jax.shard_map(local, mesh=fine, in_specs=in_specs, out_specs=P(col, row), check_vma=False)
```
